512 devices in a mesh: seq: 64 (over z, y_lo, x), head: 8 (over y_hi, core).
Axes of the slice: x: 4, y: 8 (y_hi: 4, y_lo: 2; y = y_hi * 2 + y_lo), z: 8, core: 2. Of those that a mesh axis runs over, the one named last changes fastest.
Arguments:
- queries: bfloat16 [98304, 3072], P(('seq', 'head'))
- keys: bfloat16 [98304, 3072], P(('seq', 'head'))
- values: bfloat16 [98304, 3072], P(('seq', 'head')), may hold values from -6 to 6
- neighbours: int32 [24, 768, 12], P(None, 'seq'), may hold values from 0 to 767, as said below
- counts: int32 [24, 768], P(None, 'seq'), may hold values from 1 to 12
Outputs:
- attended: bfloat16 [98304, 3072], P(('seq', 'head'))
The draws below stay inside these ranges and needn't reach their ends.
Inputs may be any that keep to these rules, and one draw needn't show every extreme that they name: `neighbours`: slot 0 names the tile itself. For head h and tile n, the slots name distinct tiles c - 6 to c + 6, where c is n clamped to the range 6 to 768 - 7.
All inputs are finite; a program needn't handle non-finite values.
Results may differ from the reference program's by a relative error of at most 0.011.
Values may be sent and summed in bfloat16 or wider, within the bound.
No kernel may reach another device: no remote copies, remote signals or barrier semaphores. Data moves between devices by JAX's collectives and lax.ppermute only.
A program may use at most 64 MiB of HBM per device.

```python
import math
import jax
import jax.numpy as jnp
from jax import lax

HEADS = 24
HD = 128
TILE = 128
NB = 12
REACH = 6
TILES_DEV = 12
NTILES = 768
TOKENS = 98304
N_SEQ = 64


def shared_keys(key):
    return jax.random.normal(jax.random.fold_in(key, 5), (TOKENS, HEADS * HD), jnp.float32)


def draw_keys(key, part):
    common = shared_keys(key)
    drawn = common
    return jnp.clip(drawn, -24.0, 24.0).astype(jnp.bfloat16)


def draw_queries(key, part):
    key = jax.random.fold_in(key, 22)
    first = jax.random.fold_in(key, 0)
    own = jax.random.normal(first, (TOKENS, HEADS * HD), jnp.float32)
    drawn = own
    return jnp.clip(drawn, -32.0, 32.0).astype(jnp.bfloat16)


def draw_neighbours(key, part):
    key = jax.random.fold_in(key, 11)
    window = 2 * REACH + 1
    tiles = jnp.arange(NTILES, dtype=jnp.int32)[None, :, None]
    centre = jnp.clip(tiles, REACH, NTILES - 1 - REACH)
    offsets = jnp.arange(window, dtype=jnp.int32)[None, None, :]
    candidate = jnp.broadcast_to(centre - REACH + offsets, (HEADS, NTILES, window))
    noise = jax.random.randint(key, (HEADS, NTILES, window), 0, 1 << 20)
    ranking = noise * window + offsets
    ranking = jnp.where(candidate == tiles, -1, ranking)
    order = jnp.argsort(ranking, axis=-1)
    picked = jnp.take_along_axis(candidate, order[:, :, :NB], axis=-1)
    return picked.astype(jnp.int32)


def draw_counts(key, part):
    key = jax.random.fold_in(key, 12)
    first, second, third, fourth = jax.random.split(key, 4)
    sparse_level = jax.random.randint(first, (HEADS,), 1, NB // 3 + 2)
    dense_pick = jax.random.randint(second, (HEADS,), 0, 4) == 0
    level = jnp.where(dense_pick, NB, sparse_level)
    shuffled = jax.random.permutation(third, HEADS)
    level = level.at[shuffled[0]].set(NB).at[shuffled[1]].set(1)
    noise = jax.random.randint(fourth, (HEADS, NTILES), -1, 2)
    noise = noise.at[:, 0].set(0)
    return jnp.clip(level[:, None] + noise, 1, NB).astype(jnp.int32)


def level_of(rng, dims, cuts, low, top_value):
    def one(axis_at, shards_of):
        heights = jax.random.uniform(jax.random.fold_in(jax.random.fold_in(rng, 6), axis_at), (shards_of,), jnp.float32, low / len(cuts), top_value / len(cuts))
        return jnp.repeat(jnp.exp(heights), dims[axis_at] // shards_of).reshape((-1,) + (1,) * (len(dims) - axis_at - 1))

    gain = one(*cuts[0])
    for cut in cuts[1:]:
        gain = gain * one(*cut)
    return gain


def gaussian(stream_key, extent, scale, bound, cuts=(), kind=jnp.bfloat16):
    factor_of = level_of(stream_key, extent, cuts, -0.22, 0.18) if cuts else 1.0
    values = jax.random.normal(stream_key, extent, jnp.float32) * scale * factor_of
    return jnp.minimum(jnp.maximum(values, -bound), bound).astype(kind)


def setup_inputs(seed: int = 0) -> dict:
    key_of = jax.random.split(jax.random.key(seed), 6)
    return {
        "queries": draw_queries(jax.random.fold_in(key_of[5], 71), 0),
        "keys": draw_keys(jax.random.fold_in(key_of[5], 71), 0),
        "values": gaussian(key_of[2], (TOKENS, HEADS * HD), 1.0, 6.0, ((0, 512),)),
        "neighbours": draw_neighbours(jax.random.fold_in(key_of[5], 71), 0),
        "counts": draw_counts(jax.random.fold_in(key_of[5], 71), 0),
    }


def sign_table(size):
    position = jnp.arange(size, dtype=jnp.int32)
    common = jnp.bitwise_and(position[:, None], position[None, :])
    parity = jnp.zeros((size, size), jnp.int32)
    for bit_level in range(max(size.bit_length() - 1, 1)):
        parity = parity + jnp.bitwise_and(jnp.right_shift(common, bit_level), 1)
    return (1 - 2 * jnp.bitwise_and(parity, 1)).astype(jnp.bfloat16)

def rotate(block, signs):
    turned = jnp.dot(block, signs, preferred_element_type=jnp.float32)
    return (turned * (1.0 / math.sqrt(HD))).astype(jnp.bfloat16)

def reference(queries, keys, values, neighbours, counts):
    signs = sign_table(HD)
    score_scale = 1.0 / math.sqrt(HD)
    slots = jnp.arange(NB, dtype=jnp.int32)

    def one_head(head_number):
        start = head_number * HD
        query_rot = rotate(lax.dynamic_slice_in_dim(queries, start, HD, 1), signs).reshape(NTILES, TILE, HD)
        key_rot = rotate(lax.dynamic_slice_in_dim(keys, start, HD, 1), signs).reshape(NTILES, TILE, HD)
        value_tiles = lax.dynamic_slice_in_dim(values, start, HD, 1).reshape(NTILES, TILE, HD)
        listed = lax.dynamic_index_in_dim(neighbours, head_number, 0, keepdims=False)
        counted = lax.dynamic_index_in_dim(counts, head_number, 0, keepdims=False)

        def one_group(group_number):
            first = group_number * TILES_DEV
            chosen = lax.dynamic_slice_in_dim(listed, first, TILES_DEV, 0)
            limit = lax.dynamic_slice_in_dim(counted, first, TILES_DEV, 0)
            query_block = lax.dynamic_slice_in_dim(query_rot, first, TILES_DEV, 0).astype(jnp.float32)
            key_block = jnp.take(key_rot, chosen, axis=0).astype(jnp.float32)
            value_block = jnp.take(value_tiles, chosen, axis=0).astype(jnp.float32)
            scores = jnp.einsum('gqd,gnkd->gqnk', query_block, key_block) * score_scale
            active = slots[None, :] < limit[:, None]
            scores = jnp.where(active[:, None, :, None], scores, -jnp.inf)
            peak = lax.optimization_barrier(jnp.max(scores, axis=(2, 3), keepdims=True))
            weights = jnp.exp(scores - peak)
            total = lax.optimization_barrier(jnp.sum(weights, axis=(2, 3)))
            rounded = lax.optimization_barrier(weights.astype(jnp.bfloat16)).astype(jnp.float32)
            mixed = jnp.einsum('gqnk,gnkd->gqd', rounded, value_block)
            return (mixed / total[:, :, None]).astype(jnp.bfloat16)
        return lax.map(one_group, jnp.arange(N_SEQ, dtype=jnp.int32)).reshape(TOKENS, HD)
    per_head = lax.map(one_head, jnp.arange(HEADS, dtype=jnp.int32))
    return jnp.transpose(per_head, (1, 0, 2)).reshape(TOKENS, HEADS * HD)
```

```python
import math

import jax
import jax.numpy as jnp
from jax import lax
from jax.experimental import pallas as pl
from jax.experimental.pallas import tpu as pltpu
from jax.sharding import PartitionSpec as P

VMEM_BYTES = 40 * 1024 * 1024


def sign_block(size):
    row = lax.broadcasted_iota(jnp.int32, (size, size), 0)
    column = lax.broadcasted_iota(jnp.int32, (size, size), 1)
    common = jnp.bitwise_and(row, column)
    parity = jnp.zeros((size, size), jnp.int32)
    for bit_level in range(max(size.bit_length() - 1, 1)):
        parity = parity + jnp.bitwise_and(jnp.right_shift(common, bit_level), 1)
    return (1 - 2 * jnp.bitwise_and(parity, 1)).astype(jnp.float32).astype(jnp.bfloat16)


def prepare(arrays, rotated, group_size, per_device, head_dim):
    tokens = arrays[0].shape[0]
    width = per_device * head_dim
    scale = 1.0 / math.sqrt(head_dim)

    def kernel(*refs):
        out_ref = refs[-1]
        signs = sign_block(head_dim)
        for index, ref in enumerate(refs[:-1]):
            for head in range(per_device):
                block = ref[:, head * head_dim : (head + 1) * head_dim]
                if rotated[index]:
                    turned = jnp.dot(block, signs, preferred_element_type=jnp.float32)
                    block = (turned * scale).astype(jnp.bfloat16)
                out_ref[0, index, head] = block

    count = len(arrays)
    return pl.pallas_call(
        kernel,
        grid=(group_size,),
        in_specs=[pl.BlockSpec((tokens, width), lambda g: (0, g))] * count,
        out_specs=pl.BlockSpec(
            (1, count, per_device, tokens, head_dim), lambda g: (g, 0, 0, 0, 0)
        ),
        out_shape=jax.ShapeDtypeStruct(
            (group_size, count, per_device, tokens, head_dim), jnp.bfloat16
        ),
        cost_estimate=pl.CostEstimate(
            flops=2 * tokens * width * group_size * head_dim * sum(rotated),
            bytes_accessed=4 * tokens * width * group_size * count,
            transcendentals=0,
        ),
    )(*arrays)


def attend(own, left, right, query, listed, counts, place, tile_len):
    sources, _, heads, tokens, head_dim = own.shape
    half = left.shape[0]
    span_sources = sources + 2 * half
    rows = sources * tokens
    span_rows = span_sources * tokens
    tiles_here = rows // tile_len
    span_tiles = span_rows // tile_len
    slots = listed.shape[1] // tiles_here
    factor = math.log2(math.e) / math.sqrt(head_dim)

    def kernel(place_ref, listed_ref, counts_ref, own_ref, left_ref, right_ref, query_ref, out_ref,
               key_buf, value_buf, query_buf, sems):
        def copies(head):
            found = []
            for index, buf in ((0, key_buf), (1, value_buf)):
                first = 0
                for ref, length in ((left_ref, half), (own_ref, sources), (right_ref, half)):
                    found.append(
                        pltpu.make_async_copy(
                            ref.at[:, index, head],
                            buf.at[head, pl.ds(first, length)],
                            sems.at[head, len(found)],
                        )
                    )
                    first += length
            found.append(
                pltpu.make_async_copy(
                    query_ref.at[:, 0, head], query_buf.at[head], sems.at[head, len(found)]
                )
            )
            return found

        for head in range(heads):
            for copy in copies(head):
                copy.start()
        first_head = place_ref[0]
        first_tile = place_ref[1]

        for head in range(heads):
            for copy in copies(head):
                copy.wait()
            key_rows = key_buf.at[head].reshape(span_rows, head_dim)
            value_rows = value_buf.at[head].reshape(span_rows, head_dim)
            query_rows = query_buf.at[head].reshape(rows, head_dim)
            row = first_head + head

            @pl.loop(0, tiles_here)
            def _(tile):
                limit = counts_ref[row, tile]
                token = pl.multiple_of(tile * tile_len, tile_len)

                def place_of(slot):
                    at = listed_ref[row, tile * slots + slot] - first_tile
                    at = jnp.clip(at, 0, span_tiles - 1)
                    return pl.ds(pl.multiple_of(at * tile_len, tile_len), tile_len)

                def work(used):
                    query_now = query_rows[pl.ds(token, tile_len), :]
                    scores = []
                    peak = None
                    places = [place_of(slot) for slot in range(used)]
                    for slot in range(0, used, 2):
                        keys_now = jnp.concatenate(
                            [key_rows[places[slot], :], key_rows[places[slot + 1], :]], axis=0
                        )
                        pair = lax.dot_general(
                            query_now, keys_now, (((1,), (1,)), ((), ())),
                            preferred_element_type=jnp.float32,
                        )
                        one, two = pair[:, :tile_len], pair[:, tile_len:]
                        if slot + 2 >= used:
                            two = jnp.where(limit >= used, two, -jnp.inf)
                        scores += [one, two]
                        larger = jnp.maximum(one, two)
                        peak = larger if peak is None else jnp.maximum(peak, larger)
                    peak = jnp.max(peak, axis=1, keepdims=True)
                    total = None
                    mixed = None
                    for slot in range(0, used, 2):
                        one = jnp.exp2((scores[slot] - peak) * factor)
                        two = jnp.exp2((scores[slot + 1] - peak) * factor)
                        both = one + two
                        total = both if total is None else total + both
                        weights = jnp.concatenate(
                            [one.astype(jnp.bfloat16), two.astype(jnp.bfloat16)], axis=1
                        )
                        values_now = jnp.concatenate(
                            [value_rows[places[slot], :], value_rows[places[slot + 1], :]], axis=0
                        )
                        update = jnp.dot(weights, values_now, preferred_element_type=jnp.float32)
                        mixed = update if mixed is None else mixed + update
                    total = jnp.sum(total, axis=1, keepdims=True)
                    out_ref[pl.ds(token, tile_len), head * head_dim : (head + 1) * head_dim] = (
                        mixed / total
                    ).astype(jnp.bfloat16)

                for used in range(2, slots + 1, 2):
                    @pl.when((limit + 1) // 2 == used // 2)
                    def _():
                        work(used)

    smem = pl.BlockSpec(memory_space=pltpu.SMEM)
    hbm = pl.BlockSpec(memory_space=pl.ANY)
    pairs = heads * tiles_here * slots
    return pl.pallas_call(
        kernel,
        in_specs=[smem, smem, smem, hbm, hbm, hbm, hbm],
        out_specs=pl.BlockSpec(memory_space=pltpu.VMEM),
        out_shape=jax.ShapeDtypeStruct((rows, heads * head_dim), jnp.bfloat16),
        scratch_shapes=[
            pltpu.VMEM((heads, span_sources, tokens, head_dim), jnp.bfloat16),
            pltpu.VMEM((heads, span_sources, tokens, head_dim), jnp.bfloat16),
            pltpu.VMEM((heads, sources, tokens, head_dim), jnp.bfloat16),
            pltpu.SemaphoreType.DMA((heads, 7)),
        ],
        compiler_params=pltpu.CompilerParams(vmem_limit_bytes=VMEM_BYTES),
        cost_estimate=pl.CostEstimate(
            flops=4 * pairs * tile_len * tile_len * head_dim,
            bytes_accessed=2 * heads * head_dim * (2 * span_rows + 2 * rows),
            transcendentals=pairs * tile_len * tile_len,
        ),
    )(place, listed, counts, own, left, right, query)


def body(queries, keys, values, neighbours, counts):
    group_size = lax.axis_size("head")
    blocks = lax.axis_size("seq")
    local_tokens, feature_width = queries.shape
    head_count, tiles_here = counts.shape
    head_dim = feature_width // head_count
    per_device = head_count // group_size
    tile_len = local_tokens * group_size // tiles_here
    half = group_size // 2
    halo_tiles = half * local_tokens // tile_len

    def exchange(array):
        return lax.all_to_all(array, "head", split_axis=0, concat_axis=0, tiled=True)

    packed = prepare([keys, values], [True, False], group_size, per_device, head_dim)
    own = exchange(packed)
    packed = prepare([queries], [True], group_size, per_device, head_dim)
    query = exchange(packed)
    up = [(i, i + 1) for i in range(blocks - 1)]
    down = [(i + 1, i) for i in range(blocks - 1)]
    left = lax.ppermute(own[group_size - half :], "seq", up)
    right = lax.ppermute(own[:half], "seq", down)
    place = jnp.stack(
        [
            lax.axis_index("head") * per_device,
            lax.axis_index("seq") * tiles_here - halo_tiles,
        ]
    ).astype(jnp.int32)
    listed = neighbours.reshape(head_count, -1)
    result = attend(own, left, right, query, listed, counts, place, tile_len)
    result = exchange(result.reshape(group_size, local_tokens, per_device * head_dim))
    return jnp.moveaxis(result, 0, 1).reshape(local_tokens, feature_width)


def solution(mesh):
    placed = (
        P(("seq", "head"), None),
        P(("seq", "head"), None),
        P(("seq", "head"), None),
        P(None, "seq", None),
        P(None, "seq"),
    )
    return jax.shard_map(
        body, mesh=mesh, in_specs=placed, out_specs=P(("seq", "head"), None), check_vma=False
    )
```

```python
import math

import jax
import jax.numpy as jnp
from jax import lax
from jax.experimental import pallas as pl
from jax.experimental.pallas import tpu as pltpu
from jax.sharding import PartitionSpec as P

VMEM_BYTES = 60 * 1024 * 1024
GROUP = 6


def sign_block(size):
    row = lax.broadcasted_iota(jnp.int32, (size, size), 0)
    column = lax.broadcasted_iota(jnp.int32, (size, size), 1)
    common = jnp.bitwise_and(row, column)
    parity = jnp.zeros((size, size), jnp.int32)
    for bit_level in range(max(size.bit_length() - 1, 1)):
        parity = parity + jnp.bitwise_and(jnp.right_shift(common, bit_level), 1)
    return (1 - 2 * jnp.bitwise_and(parity, 1)).astype(jnp.float32).astype(jnp.bfloat16)


def prepare(arrays, rotated, group_size, per_device, head_dim):
    tokens, width = arrays[0].shape
    count = len(arrays)
    step = tokens // 2
    scale = 1.0 / math.sqrt(head_dim)

    def kernel(*refs):
        out_ref, sign_ref = refs[-2:]

        @pl.when(pl.program_id(0) == 0)
        def _():
            sign_ref[...] = sign_block(head_dim)

        for index, ref in enumerate(refs[:-2]):
            for group in range(group_size):
                for head in range(per_device):
                    column = (group * per_device + head) * head_dim
                    block = ref[:, column : column + head_dim]
                    if rotated[index]:
                        turned = jnp.dot(block, sign_ref[...], preferred_element_type=jnp.float32)
                        block = (turned * scale).astype(jnp.bfloat16)
                    out_ref[group, index, head] = block

    return pl.pallas_call(
        kernel,
        grid=(tokens // step,),
        in_specs=[pl.BlockSpec((step, width), lambda g: (g, 0))] * count,
        out_specs=pl.BlockSpec(
            (group_size, count, per_device, step, head_dim), lambda g: (0, 0, 0, g, 0)
        ),
        out_shape=jax.ShapeDtypeStruct(
            (group_size, count, per_device, tokens, head_dim), jnp.bfloat16
        ),
        scratch_shapes=[pltpu.VMEM((head_dim, head_dim), jnp.bfloat16)],
        compiler_params=pltpu.CompilerParams(vmem_limit_bytes=VMEM_BYTES),
        cost_estimate=pl.CostEstimate(
            flops=2 * tokens * width * head_dim * sum(rotated),
            bytes_accessed=4 * tokens * width * count,
            transcendentals=0,
        ),
    )(*arrays)


def attend(own, left, right, query, listed, counts, place, tile_len):
    sources, _, heads, tokens, head_dim = own.shape
    half = left.shape[0]
    span_sources = sources + 2 * half
    rows = sources * tokens
    span_rows = span_sources * tokens
    tiles_here = rows // tile_len
    span_tiles = span_rows // tile_len
    slots = listed.shape[1] // tiles_here
    factor = math.log2(math.e) / math.sqrt(head_dim)

    def kernel(place_ref, listed_ref, counts_ref, own_ref, left_ref, right_ref, query_ref, out_ref,
               key_buf, value_buf, query_buf, sems):
        def copies(head):
            found = []
            for index, buf in ((0, key_buf), (1, value_buf)):
                first = 0
                for ref, length in ((left_ref, half), (own_ref, sources), (right_ref, half)):
                    found.append(
                        pltpu.make_async_copy(
                            ref.at[:, index, head],
                            buf.at[head, pl.ds(first, length)],
                            sems.at[head, len(found)],
                        )
                    )
                    first += length
            found.append(
                pltpu.make_async_copy(
                    query_ref.at[:, 0, head], query_buf.at[head], sems.at[head, len(found)]
                )
            )
            return found

        for head in range(heads):
            for copy in copies(head):
                copy.start()
        first_head = place_ref[0]
        first_tile = place_ref[1]

        @pl.loop(0, heads)
        def _(head):
            for copy in copies(head):
                copy.wait()
            key_rows = key_buf.at[head].reshape(span_rows, head_dim)
            value_rows = value_buf.at[head].reshape(span_rows, head_dim)
            query_rows = query_buf.at[head].reshape(rows, head_dim)
            row = first_head + head
            column = pl.ds(pl.multiple_of(head * head_dim, head_dim), head_dim)

            @pl.loop(0, tiles_here // GROUP)
            def _(group):
                tiles = [group * GROUP + member for member in range(GROUP)]
                limits = [counts_ref[row, tile] for tile in tiles]
                most = limits[0]
                for limit in limits[1:]:
                    most = jnp.maximum(most, limit)

                def place_of(tile, slot):
                    at = listed_ref[row, tile * slots + slot] - first_tile
                    at = jnp.clip(at, 0, span_tiles - 1)
                    return pl.ds(pl.multiple_of(at * tile_len, tile_len), tile_len)

                def first_part(tile, limit, used):
                    token = pl.multiple_of(tile * tile_len, tile_len)
                    query_now = query_rows[pl.ds(token, tile_len), :]
                    scores = []
                    peak = None
                    places = [place_of(tile, slot) for slot in range(used)]
                    for slot in range(0, used, 2):
                        keys_now = jnp.concatenate(
                            [key_rows[places[slot], :], key_rows[places[slot + 1], :]], axis=0
                        )
                        pair = lax.dot_general(
                            query_now, keys_now, (((1,), (1,)), ((), ())),
                            preferred_element_type=jnp.float32,
                        )
                        one, two = pair[:, :tile_len], pair[:, tile_len:]
                        if slot > 0:
                            one = jnp.where(limit > slot, one, -jnp.inf)
                        two = jnp.where(limit > slot + 1, two, -jnp.inf)
                        scores += [one, two]
                        larger = jnp.maximum(one, two)
                        peak = larger if peak is None else jnp.maximum(peak, larger)
                    return places, scores, jnp.max(peak, axis=1, keepdims=True)

                def second_part(tile, places, scores, peak):
                    token = pl.multiple_of(tile * tile_len, tile_len)
                    total = None
                    mixed = None
                    for slot in range(0, len(places), 2):
                        one = jnp.exp2((scores[slot] - peak) * factor)
                        two = jnp.exp2((scores[slot + 1] - peak) * factor)
                        both = one + two
                        total = both if total is None else total + both
                        weights = jnp.concatenate(
                            [one.astype(jnp.bfloat16), two.astype(jnp.bfloat16)], axis=1
                        )
                        values_now = jnp.concatenate(
                            [value_rows[places[slot], :], value_rows[places[slot + 1], :]], axis=0
                        )
                        update = jnp.dot(weights, values_now, preferred_element_type=jnp.float32)
                        mixed = update if mixed is None else mixed + update
                    total = jnp.sum(total, axis=1, keepdims=True)
                    out_ref[pl.ds(token, tile_len), column] = (mixed / total).astype(jnp.bfloat16)

                for used in range(2, slots + 1, 2):
                    @pl.when((most + 1) // 2 == used // 2)
                    def _():
                        parts = [first_part(t, limit, used) for t, limit in zip(tiles, limits)]
                        for tile, part in zip(tiles, parts):
                            second_part(tile, *part)

    smem = pl.BlockSpec(memory_space=pltpu.SMEM)
    hbm = pl.BlockSpec(memory_space=pl.ANY)
    pairs = heads * tiles_here * slots
    return pl.pallas_call(
        kernel,
        in_specs=[smem, smem, smem, hbm, hbm, hbm, hbm],
        out_specs=pl.BlockSpec(memory_space=pltpu.VMEM),
        out_shape=jax.ShapeDtypeStruct((rows, heads * head_dim), jnp.bfloat16),
        scratch_shapes=[
            pltpu.VMEM((heads, span_sources, tokens, head_dim), jnp.bfloat16),
            pltpu.VMEM((heads, span_sources, tokens, head_dim), jnp.bfloat16),
            pltpu.VMEM((heads, sources, tokens, head_dim), jnp.bfloat16),
            pltpu.SemaphoreType.DMA((heads, 7)),
        ],
        compiler_params=pltpu.CompilerParams(vmem_limit_bytes=VMEM_BYTES),
        cost_estimate=pl.CostEstimate(
            flops=4 * pairs * tile_len * tile_len * head_dim,
            bytes_accessed=2 * heads * head_dim * (2 * span_rows + 2 * rows),
            transcendentals=pairs * tile_len * tile_len,
        ),
    )(place, listed, counts, own, left, right, query)


def body(queries, keys, values, neighbours, counts):
    group_size = lax.axis_size("head")
    blocks = lax.axis_size("seq")
    local_tokens, feature_width = queries.shape
    head_count, tiles_here = counts.shape
    head_dim = feature_width // head_count
    per_device = head_count // group_size
    tile_len = local_tokens * group_size // tiles_here
    half = group_size // 2
    halo_tiles = half * local_tokens // tile_len

    def exchange(array):
        return lax.all_to_all(array, "head", split_axis=0, concat_axis=0, tiled=True)

    packed = prepare([keys, values], [True, False], group_size, per_device, head_dim)
    own = exchange(packed)
    packed = prepare([queries], [True], group_size, per_device, head_dim)
    query = exchange(packed)
    up = [(i, i + 1) for i in range(blocks - 1)]
    down = [(i + 1, i) for i in range(blocks - 1)]
    left = lax.ppermute(own[group_size - half :], "seq", up)
    right = lax.ppermute(own[:half], "seq", down)
    place = jnp.stack(
        [
            lax.axis_index("head") * per_device,
            lax.axis_index("seq") * tiles_here - halo_tiles,
        ]
    ).astype(jnp.int32)
    listed = neighbours.reshape(head_count, -1)
    result = attend(own, left, right, query, listed, counts, place, tile_len)
    result = exchange(result.reshape(group_size, local_tokens, per_device * head_dim))
    return jnp.moveaxis(result, 0, 1).reshape(local_tokens, feature_width)


def solution(mesh):
    placed = (
        P(("seq", "head"), None),
        P(("seq", "head"), None),
        P(("seq", "head"), None),
        P(None, "seq", None),
        P(None, "seq"),
    )
    return jax.shard_map(
        body, mesh=mesh, in_specs=placed, out_specs=P(("seq", "head"), None), check_vma=False
    )
```

```python
import math

import jax
import jax.numpy as jnp
from jax import lax
from jax.experimental import pallas as pl
from jax.experimental.pallas import tpu as pltpu
from jax.sharding import PartitionSpec as P

VMEM_BYTES = 60 * 1024 * 1024
GROUP = 6
ROW = 4


def sign_block(size):
    row = lax.broadcasted_iota(jnp.int32, (size, size), 0)
    column = lax.broadcasted_iota(jnp.int32, (size, size), 1)
    common = jnp.bitwise_and(row, column)
    parity = jnp.zeros((size, size), jnp.int32)
    for bit_level in range(max(size.bit_length() - 1, 1)):
        parity = parity + jnp.bitwise_and(jnp.right_shift(common, bit_level), 1)
    return (1 - 2 * jnp.bitwise_and(parity, 1)).astype(jnp.float32).astype(jnp.bfloat16)


def odd_row(block):
    return (block // ROW) % 2


def owner_block(member, odd, group_size):
    return ((member // 2 + (member % 2) * odd) % (group_size // 2)) * 2 + member % 2


def owner_of(block, head_block, group_size):
    shift = (head_block % 2) * odd_row(block)
    return ((head_block // 2 - shift) % (group_size // 2)) * 2 + head_block % 2


def prepare(arrays, rotated, group_size, per_device, head_dim):
    tokens, width = arrays[0].shape
    count = len(arrays)
    step = tokens // 2
    scale = 1.0 / math.sqrt(head_dim)

    def kernel(*refs):
        out_ref, sign_ref = refs[-2:]

        @pl.when(pl.program_id(0) == 0)
        def _():
            sign_ref[...] = sign_block(head_dim)

        odd = odd_row(lax.axis_index("seq"))
        for index, ref in enumerate(refs[:-2]):
            for group in range(group_size):
                first = owner_block(group, odd, group_size) * per_device
                for head in range(per_device):
                    column = pl.multiple_of((first + head) * head_dim, head_dim)
                    block = ref[:, pl.ds(column, head_dim)]
                    if rotated[index]:
                        turned = jnp.dot(block, sign_ref[...], preferred_element_type=jnp.float32)
                        block = (turned * scale).astype(jnp.bfloat16)
                    out_ref[group, index, head] = block

    return pl.pallas_call(
        kernel,
        grid=(tokens // step,),
        in_specs=[pl.BlockSpec((step, width), lambda g: (g, 0))] * count,
        out_specs=pl.BlockSpec(
            (group_size, count, per_device, step, head_dim), lambda g: (0, 0, 0, g, 0)
        ),
        out_shape=jax.ShapeDtypeStruct(
            (group_size, count, per_device, tokens, head_dim), jnp.bfloat16
        ),
        scratch_shapes=[pltpu.VMEM((head_dim, head_dim), jnp.bfloat16)],
        compiler_params=pltpu.CompilerParams(vmem_limit_bytes=VMEM_BYTES),
        cost_estimate=pl.CostEstimate(
            flops=2 * tokens * width * head_dim * sum(rotated),
            bytes_accessed=4 * tokens * width * count,
            transcendentals=0,
        ),
    )(*arrays)


def attend(own, left, right, query, listed, counts, place, tile_len):
    sources, _, heads, tokens, head_dim = own.shape
    half = left.shape[0]
    span_sources = sources + 2 * half
    rows = sources * tokens
    span_rows = span_sources * tokens
    tiles_here = rows // tile_len
    span_tiles = span_rows // tile_len
    slots = listed.shape[1] // tiles_here
    factor = math.log2(math.e) / math.sqrt(head_dim)

    def kernel(place_ref, listed_ref, counts_ref, own_ref, left_ref, right_ref, query_ref, out_ref,
               key_buf, value_buf, query_buf, sems):
        def copies(head):
            found = []
            for index, buf in ((0, key_buf), (1, value_buf)):
                first = 0
                for ref, length in ((left_ref, half), (own_ref, sources), (right_ref, half)):
                    found.append(
                        pltpu.make_async_copy(
                            ref.at[:, index, head],
                            buf.at[head, pl.ds(first, length)],
                            sems.at[head, len(found)],
                        )
                    )
                    first += length
            found.append(
                pltpu.make_async_copy(
                    query_ref.at[:, 0, head], query_buf.at[head], sems.at[head, len(found)]
                )
            )
            return found

        for head in range(heads):
            for copy in copies(head):
                copy.start()
        first_head = place_ref[0]
        first_tile = place_ref[1]

        @pl.loop(0, heads)
        def _(head):
            for copy in copies(head):
                copy.wait()
            key_rows = key_buf.at[head].reshape(span_rows, head_dim)
            value_rows = value_buf.at[head].reshape(span_rows, head_dim)
            query_rows = query_buf.at[head].reshape(rows, head_dim)
            row = first_head + head
            column = pl.ds(pl.multiple_of(head * head_dim, head_dim), head_dim)

            @pl.loop(0, tiles_here // GROUP)
            def _(group):
                tiles = [group * GROUP + member for member in range(GROUP)]
                limits = [counts_ref[row, tile] for tile in tiles]
                most = limits[0]
                for limit in limits[1:]:
                    most = jnp.maximum(most, limit)

                def place_of(tile, slot):
                    at = listed_ref[row, tile * slots + slot] - first_tile
                    at = jnp.clip(at, 0, span_tiles - 1)
                    return pl.ds(pl.multiple_of(at * tile_len, tile_len), tile_len)

                def first_part(tile, limit, used):
                    token = pl.multiple_of(tile * tile_len, tile_len)
                    query_now = query_rows[pl.ds(token, tile_len), :]
                    scores = []
                    peak = None
                    places = [place_of(tile, slot) for slot in range(used)]
                    for slot in range(0, used, 2):
                        keys_now = jnp.concatenate(
                            [key_rows[places[slot], :], key_rows[places[slot + 1], :]], axis=0
                        )
                        pair = lax.dot_general(
                            query_now, keys_now, (((1,), (1,)), ((), ())),
                            preferred_element_type=jnp.float32,
                        )
                        one, two = pair[:, :tile_len], pair[:, tile_len:]
                        if slot > 0:
                            one = jnp.where(limit > slot, one, -jnp.inf)
                        two = jnp.where(limit > slot + 1, two, -jnp.inf)
                        scores += [one, two]
                        larger = jnp.maximum(one, two)
                        peak = larger if peak is None else jnp.maximum(peak, larger)
                    return places, scores, jnp.max(peak, axis=1, keepdims=True)

                def second_part(tile, places, scores, peak):
                    token = pl.multiple_of(tile * tile_len, tile_len)
                    total = None
                    mixed = None
                    for slot in range(0, len(places), 2):
                        one = jnp.exp2((scores[slot] - peak) * factor)
                        two = jnp.exp2((scores[slot + 1] - peak) * factor)
                        both = one + two
                        total = both if total is None else total + both
                        weights = jnp.concatenate(
                            [one.astype(jnp.bfloat16), two.astype(jnp.bfloat16)], axis=1
                        )
                        values_now = jnp.concatenate(
                            [value_rows[places[slot], :], value_rows[places[slot + 1], :]], axis=0
                        )
                        update = jnp.dot(weights, values_now, preferred_element_type=jnp.float32)
                        mixed = update if mixed is None else mixed + update
                    total = jnp.sum(total, axis=1, keepdims=True)
                    out_ref[pl.ds(token, tile_len), column] = (mixed / total).astype(jnp.bfloat16)

                for used in range(2, slots + 1, 2):
                    @pl.when((most + 1) // 2 == used // 2)
                    def _():
                        parts = [first_part(t, limit, used) for t, limit in zip(tiles, limits)]
                        for tile, part in zip(tiles, parts):
                            second_part(tile, *part)

    smem = pl.BlockSpec(memory_space=pltpu.SMEM)
    hbm = pl.BlockSpec(memory_space=pl.ANY)
    pairs = heads * tiles_here * slots
    return pl.pallas_call(
        kernel,
        in_specs=[smem, smem, smem, hbm, hbm, hbm, hbm],
        out_specs=pl.BlockSpec(memory_space=pltpu.VMEM),
        out_shape=jax.ShapeDtypeStruct((rows, heads * head_dim), jnp.bfloat16),
        scratch_shapes=[
            pltpu.VMEM((heads, span_sources, tokens, head_dim), jnp.bfloat16),
            pltpu.VMEM((heads, span_sources, tokens, head_dim), jnp.bfloat16),
            pltpu.VMEM((heads, sources, tokens, head_dim), jnp.bfloat16),
            pltpu.SemaphoreType.DMA((heads, 7)),
        ],
        compiler_params=pltpu.CompilerParams(vmem_limit_bytes=VMEM_BYTES),
        cost_estimate=pl.CostEstimate(
            flops=4 * pairs * tile_len * tile_len * head_dim,
            bytes_accessed=2 * heads * head_dim * (2 * span_rows + 2 * rows),
            transcendentals=pairs * tile_len * tile_len,
        ),
    )(place, listed, counts, own, left, right, query)


def assemble(parts):
    members, tokens, width = parts.shape
    step = tokens // 2

    def kernel(parts_ref, out_ref):
        odd = odd_row(lax.axis_index("seq"))
        for member in range(members):
            column = pl.multiple_of(owner_block(member, odd, members) * width, width)
            out_ref[:, pl.ds(column, width)] = parts_ref[member]

    return pl.pallas_call(
        kernel,
        grid=(tokens // step,),
        in_specs=[pl.BlockSpec((members, step, width), lambda g: (0, g, 0))],
        out_specs=pl.BlockSpec((step, members * width), lambda g: (g, 0)),
        out_shape=jax.ShapeDtypeStruct((tokens, members * width), parts.dtype),
        compiler_params=pltpu.CompilerParams(vmem_limit_bytes=VMEM_BYTES),
        cost_estimate=pl.CostEstimate(
            flops=0, bytes_accessed=4 * tokens * members * width, transcendentals=0
        ),
    )(parts)


def body(queries, keys, values, neighbours, counts):
    group_size = lax.axis_size("head")
    blocks = lax.axis_size("seq")
    local_tokens, feature_width = queries.shape
    head_count, tiles_here = counts.shape
    head_dim = feature_width // head_count
    per_device = head_count // group_size
    tile_len = local_tokens * group_size // tiles_here
    half = group_size // 2
    halo_tiles = half * local_tokens // tile_len

    def exchange(array):
        return lax.all_to_all(array, "head", split_axis=0, concat_axis=0, tiled=True)

    packed = prepare([keys, values], [True, False], group_size, per_device, head_dim)
    own = exchange(packed)
    packed = prepare([queries], [True], group_size, per_device, head_dim)
    query = exchange(packed)
    up = [
        tuple(
            at * group_size + owner_of(at, head_block, group_size) for at in (block, block + 1)
        )
        for block in range(blocks - 1)
        for head_block in range(group_size)
    ]
    down = [(there, here) for here, there in up]
    left = lax.ppermute(own[group_size - half :], ("seq", "head"), up)
    right = lax.ppermute(own[:half], ("seq", "head"), down)
    row_is_odd = odd_row(lax.axis_index("seq"))
    place = jnp.stack(
        [
            owner_block(lax.axis_index("head"), row_is_odd, group_size) * per_device,
            lax.axis_index("seq") * tiles_here - halo_tiles,
        ]
    ).astype(jnp.int32)
    listed = neighbours.reshape(head_count, -1)
    result = attend(own, left, right, query, listed, counts, place, tile_len)
    result = exchange(result.reshape(group_size, local_tokens, per_device * head_dim))
    return assemble(result)


def solution(mesh):
    placed = (
        P(("seq", "head"), None),
        P(("seq", "head"), None),
        P(("seq", "head"), None),
        P(None, "seq", None),
        P(None, "seq"),
    )
    return jax.shard_map(
        body, mesh=mesh, in_specs=placed, out_specs=P(("seq", "head"), None), check_vma=False
    )
```

```python
import math

import jax
import jax.numpy as jnp
from jax import lax
from jax.experimental import pallas as pl
from jax.experimental.pallas import tpu as pltpu
from jax.sharding import PartitionSpec as P

VMEM_BYTES = 60 * 1024 * 1024
GROUP = 6
HALO_SLOTS = 8


def sign_block(size):
    row = lax.broadcasted_iota(jnp.int32, (size, size), 0)
    column = lax.broadcasted_iota(jnp.int32, (size, size), 1)
    common = jnp.bitwise_and(row, column)
    parity = jnp.zeros((size, size), jnp.int32)
    for bit_level in range(max(size.bit_length() - 1, 1)):
        parity = parity + jnp.bitwise_and(jnp.right_shift(common, bit_level), 1)
    return (1 - 2 * jnp.bitwise_and(parity, 1)).astype(jnp.float32).astype(jnp.bfloat16)


def prepare(arrays, rotated, group_size, per_device, head_dim):
    tokens, width = arrays[0].shape
    count = len(arrays)
    step = tokens // 2
    scale = 1.0 / math.sqrt(head_dim)

    def kernel(*refs):
        out_ref, sign_ref = refs[-2:]

        @pl.when(pl.program_id(0) == 0)
        def _():
            sign_ref[...] = sign_block(head_dim)

        for index, ref in enumerate(refs[:-2]):
            for group in range(group_size):
                for head in range(per_device):
                    column = (group * per_device + head) * head_dim
                    block = ref[:, column : column + head_dim]
                    if rotated[index]:
                        turned = jnp.dot(block, sign_ref[...], preferred_element_type=jnp.float32)
                        block = (turned * scale).astype(jnp.bfloat16)
                    out_ref[group, index, head] = block

    return pl.pallas_call(
        kernel,
        grid=(tokens // step,),
        in_specs=[pl.BlockSpec((step, width), lambda g: (g, 0))] * count,
        out_specs=pl.BlockSpec(
            (group_size, count, per_device, step, head_dim), lambda g: (0, 0, 0, g, 0)
        ),
        out_shape=jax.ShapeDtypeStruct(
            (group_size, count, per_device, tokens, head_dim), jnp.bfloat16
        ),
        scratch_shapes=[pltpu.VMEM((head_dim, head_dim), jnp.bfloat16)],
        compiler_params=pltpu.CompilerParams(vmem_limit_bytes=VMEM_BYTES),
        cost_estimate=pl.CostEstimate(
            flops=2 * tokens * width * head_dim * sum(rotated),
            bytes_accessed=4 * tokens * width * count,
            transcendentals=0,
        ),
    )(*arrays)


def scores_of(query_now, keys_of, limit, first_active):
    scores = []
    largest = None
    for slot in range(0, len(keys_of), 2):
        keys_now = jnp.concatenate([keys_of[slot](), keys_of[slot + 1]()], axis=0)
        pair = lax.dot_general(
            query_now, keys_now, (((1,), (1,)), ((), ())), preferred_element_type=jnp.float32
        )
        half = pair.shape[1] // 2
        one, two = pair[:, :half], pair[:, half:]
        if slot >= first_active:
            one = jnp.where(limit > slot, one, -jnp.inf)
        two = jnp.where(limit > slot + 1, two, -jnp.inf)
        scores += [one, two]
        larger = jnp.maximum(one, two)
        largest = larger if largest is None else jnp.maximum(largest, larger)
    return scores, largest


def mix(scores, level, factor, values_of):
    total = None
    mixed = None
    for slot in range(0, len(scores), 2):
        one = jnp.exp2(scores[slot] * factor - level)
        two = jnp.exp2(scores[slot + 1] * factor - level)
        both = one + two
        total = both if total is None else total + both
        weights = jnp.concatenate([one.astype(jnp.bfloat16), two.astype(jnp.bfloat16)], axis=1)
        values_now = jnp.concatenate([values_of[slot](), values_of[slot + 1]()], axis=0)
        update = jnp.dot(weights, values_now, preferred_element_type=jnp.float32)
        mixed = update if mixed is None else mixed + update
    return jnp.sum(total, axis=1, keepdims=True), mixed


def tile_rows(ref, at, count, tile_len):
    at = jnp.clip(at, 0, count - 1)
    return lambda: ref[pl.ds(pl.multiple_of(at * tile_len, tile_len), tile_len), :]


def attend_local(own, listed, counts, place, tile_len, reach):
    sources, _, heads, tokens, head_dim = own.shape
    rows = sources * tokens
    tiles_here = rows // tile_len
    slots = listed.shape[1] // tiles_here
    factor = math.log2(math.e) / math.sqrt(head_dim)
    group_count = tiles_here // GROUP

    def kernel(place_ref, listed_ref, counts_ref, own_ref, mixed_ref, stats_ref, halo_ref,
               buf, inside_ref, sems):
        def copies(head):
            return [
                pltpu.make_async_copy(
                    own_ref.at[:, index, head], buf.at[index, head], sems.at[head, index]
                )
                for index in range(3)
            ]

        for head in range(heads):
            for copy in copies(head):
                copy.start()
        first_head = place_ref[0]
        first_tile = place_ref[1]
        for member in range(GROUP):
            for slot in range(slots):
                inside_ref[member, slot] = 0

        @pl.loop(0, heads)
        def _(head):
            for copy in copies(head):
                copy.wait()
            key_rows, value_rows, query_rows = [
                buf.at[index, head].reshape(rows, head_dim) for index in range(3)
            ]
            row = first_head + head
            column = pl.ds(pl.multiple_of(head * head_dim, head_dim), head_dim)

            @pl.loop(0, group_count)
            def _(group):
                tiles = [group * GROUP + member for member in range(GROUP)]
                limits = []
                for member, tile in enumerate(tiles):
                    limit = counts_ref[row, tile]
                    line = head * tiles_here + tile
                    inside = jnp.int32(0)
                    outside = jnp.int32(0)
                    for spare in range(HALO_SLOTS):
                        halo_ref[line, spare] = 0
                    for slot in range(slots):
                        at = listed_ref[row, tile * slots + slot] - first_tile
                        active = slot < limit
                        is_inside = (at >= 0) & (at < tiles_here)
                        inside_ref[member, inside] = at
                        halo_ref[line, jnp.minimum(outside, HALO_SLOTS - 2)] = jnp.where(
                            at < 0, at + reach, at - tiles_here + reach
                        )
                        inside = inside + (active & is_inside).astype(jnp.int32)
                        outside = outside + (active & ~is_inside).astype(jnp.int32)
                    halo_ref[line, HALO_SLOTS - 1] = outside
                    limits.append(inside)
                most = limits[0]
                for limit in limits[1:]:
                    most = jnp.maximum(most, limit)

                def work(used):
                    begun = []
                    for member, tile in enumerate(tiles):
                        token = pl.multiple_of(tile * tile_len, tile_len)
                        query_now = query_rows[pl.ds(token, tile_len), :]
                        places = [inside_ref[member, slot] for slot in range(used)]
                        scores, largest = scores_of(
                            query_now,
                            [tile_rows(key_rows, at, tiles_here, tile_len) for at in places],
                            limits[member],
                            1,
                        )
                        begun.append((token, places, scores, jnp.max(largest, axis=1, keepdims=True)))
                    for token, places, scores, peak in begun:
                        total, mixed = mix(
                            scores,
                            peak * factor,
                            factor,
                            [tile_rows(value_rows, at, tiles_here, tile_len) for at in places],
                        )
                        mixed_ref[pl.ds(token, tile_len), column] = mixed / total
                        level = peak * factor + jnp.log2(total)
                        stats_ref[pl.ds(token, tile_len), column] = jnp.broadcast_to(
                            level, (tile_len, head_dim)
                        )

                for used in range(2, slots + 1, 2):
                    @pl.when((most + 1) // 2 == used // 2)
                    def _():
                        work(used)

    smem = pl.BlockSpec(memory_space=pltpu.SMEM)
    vmem = pl.BlockSpec(memory_space=pltpu.VMEM)
    pairs = heads * tiles_here * slots
    state = jax.ShapeDtypeStruct((rows, heads * head_dim), jnp.float32)
    return pl.pallas_call(
        kernel,
        in_specs=[smem, smem, smem, pl.BlockSpec(memory_space=pl.ANY)],
        out_specs=[vmem, vmem, smem],
        out_shape=[state, state, jax.ShapeDtypeStruct((heads * tiles_here, HALO_SLOTS), jnp.int32)],
        scratch_shapes=[
            pltpu.VMEM((3, heads, sources, tokens, head_dim), jnp.bfloat16),
            pltpu.SMEM((GROUP, slots), jnp.int32),
            pltpu.SemaphoreType.DMA((heads, 3)),
        ],
        compiler_params=pltpu.CompilerParams(vmem_limit_bytes=VMEM_BYTES // 3),
        cost_estimate=pl.CostEstimate(
            flops=4 * pairs * tile_len * tile_len * head_dim,
            bytes_accessed=2 * heads * head_dim * 7 * rows,
            transcendentals=pairs * tile_len * tile_len,
        ),
    )(place, listed, counts, own)


def attend_halo(own, left, right, mixed, stats, halo, tile_len):
    sources, _, heads, tokens, head_dim = own.shape
    half = left.shape[0]
    rows = sources * tokens
    halo_rows = 2 * half * tokens
    halo_tiles = halo_rows // tile_len
    tiles_here = rows // tile_len
    factor = math.log2(math.e) / math.sqrt(head_dim)

    def kernel(halo_ref, own_ref, left_ref, right_ref, mixed_ref, stats_ref, out_ref,
               buf, query_buf, sems):
        def copies(head):
            pairs = [(own_ref.at[:, 2, head], query_buf.at[head])]
            for index in range(2):
                pairs.append((left_ref.at[:, index, head], buf.at[index, head, pl.ds(0, half)]))
                pairs.append((right_ref.at[:, index, head], buf.at[index, head, pl.ds(half, half)]))
            return [
                pltpu.make_async_copy(there, here, sems.at[head, number])
                for number, (there, here) in enumerate(pairs)
            ]

        for head in range(heads):
            for copy in copies(head):
                copy.start()

        @pl.loop(0, heads)
        def _(head):
            for copy in copies(head):
                copy.wait()
            key_rows, value_rows = [
                buf.at[index, head].reshape(halo_rows, head_dim) for index in range(2)
            ]
            query_rows = query_buf.at[head].reshape(rows, head_dim)
            column = pl.ds(pl.multiple_of(head * head_dim, head_dim), head_dim)

            @pl.loop(0, tiles_here // 4)
            def _(group):
                last = tiles_here - 1
                tiles = [2 * group, 2 * group + 1, last - 2 * group, last - 1 - 2 * group]
                lines = [head * tiles_here + tile for tile in tiles]
                limits = [halo_ref[line, HALO_SLOTS - 1] for line in lines]
                most = limits[0]
                for limit in limits[1:]:
                    most = jnp.maximum(most, limit)

                def work(used):
                    begun = []
                    for line, tile, limit in zip(lines, tiles, limits):
                        here = pl.ds(pl.multiple_of(tile * tile_len, tile_len), tile_len)
                        if not used:
                            out_ref[here, column] = mixed_ref[here, column].astype(jnp.bfloat16)
                            continue
                        places = [halo_ref[line, slot] for slot in range(used)]
                        scores, largest = scores_of(
                            query_rows[here, :],
                            [tile_rows(key_rows, at, halo_tiles, tile_len) for at in places],
                            limit,
                            0,
                        )
                        level = stats_ref[here, column]
                        newest = jnp.maximum(level, jnp.max(largest, axis=1, keepdims=True) * factor)
                        begun.append((here, places, scores, newest, jnp.exp2(level - newest)))
                    for here, places, scores, newest, fade in begun:
                        added, update = mix(
                            scores,
                            newest,
                            factor,
                            [tile_rows(value_rows, at, halo_tiles, tile_len) for at in places],
                        )
                        out_ref[here, column] = (
                            (mixed_ref[here, column] * fade + update) / (fade + added)
                        ).astype(jnp.bfloat16)

                for used in range(0, HALO_SLOTS - 1, 2):
                    @pl.when((most + 1) // 2 == used // 2)
                    def _():
                        work(used)

    smem = pl.BlockSpec(memory_space=pltpu.SMEM)
    hbm = pl.BlockSpec(memory_space=pl.ANY)
    vmem = pl.BlockSpec(memory_space=pltpu.VMEM)
    pairs = heads * tiles_here * (HALO_SLOTS - 2) // 2
    return pl.pallas_call(
        kernel,
        in_specs=[smem, hbm, hbm, hbm, vmem, vmem],
        out_specs=vmem,
        out_shape=jax.ShapeDtypeStruct((rows, heads * head_dim), jnp.bfloat16),
        scratch_shapes=[
            pltpu.VMEM((2, heads, 2 * half, tokens, head_dim), jnp.bfloat16),
            pltpu.VMEM((heads, sources, tokens, head_dim), jnp.bfloat16),
            pltpu.SemaphoreType.DMA((heads, 5)),
        ],
        compiler_params=pltpu.CompilerParams(vmem_limit_bytes=VMEM_BYTES // 3),
        cost_estimate=pl.CostEstimate(
            flops=4 * pairs * tile_len * tile_len * head_dim,
            bytes_accessed=2 * heads * head_dim * (2 * halo_rows + 6 * rows),
            transcendentals=pairs * tile_len * tile_len,
        ),
    )(halo, own, left, right, mixed, stats)


def body(queries, keys, values, neighbours, counts):
    group_size = lax.axis_size("head")
    blocks = lax.axis_size("seq")
    local_tokens, feature_width = queries.shape
    head_count, tiles_here = counts.shape
    head_dim = feature_width // head_count
    per_device = head_count // group_size
    tile_len = local_tokens * group_size // tiles_here
    half = group_size // 2
    halo_tiles = half * local_tokens // tile_len

    def exchange(array):
        return lax.all_to_all(array, "head", split_axis=0, concat_axis=0, tiled=True)

    packed = prepare([keys, values, queries], [True, False, True], group_size, per_device, head_dim)
    own = exchange(packed)
    up = [(i, i + 1) for i in range(blocks - 1)]
    down = [(i + 1, i) for i in range(blocks - 1)]
    left = lax.ppermute(own[group_size - half :, :2], "seq", up)
    right = lax.ppermute(own[:half, :2], "seq", down)
    place = jnp.stack(
        [lax.axis_index("head") * per_device, lax.axis_index("seq") * tiles_here]
    ).astype(jnp.int32)
    listed = neighbours.reshape(head_count, -1)
    mixed, stats, halo = attend_local(own, listed, counts, place, tile_len, halo_tiles)
    result = attend_halo(own, left, right, mixed, stats, halo, tile_len)
    result = exchange(result.reshape(group_size, local_tokens, per_device * head_dim))
    return jnp.moveaxis(result, 0, 1).reshape(local_tokens, feature_width)


def solution(mesh):
    placed = (
        P(("seq", "head"), None),
        P(("seq", "head"), None),
        P(("seq", "head"), None),
        P(None, "seq", None),
        P(None, "seq"),
    )
    return jax.shard_map(
        body, mesh=mesh, in_specs=placed, out_specs=P(("seq", "head"), None), check_vma=False
    )
```

```python
import math

import jax
import jax.numpy as jnp
from jax import lax
from jax.experimental import pallas as pl
from jax.experimental.pallas import tpu as pltpu
from jax.sharding import PartitionSpec as P

VMEM_BYTES = 60 * 1024 * 1024
OWN_SLOTS = 16
HALO_SLOTS = 8


def sign_block(size):
    row = lax.broadcasted_iota(jnp.int32, (size, size), 0)
    column = lax.broadcasted_iota(jnp.int32, (size, size), 1)
    common = jnp.bitwise_and(row, column)
    parity = jnp.zeros((size, size), jnp.int32)
    for bit_level in range(max(size.bit_length() - 1, 1)):
        parity = parity + jnp.bitwise_and(jnp.right_shift(common, bit_level), 1)
    return (1 - 2 * jnp.bitwise_and(parity, 1)).astype(jnp.float32).astype(jnp.bfloat16)


def prepare(arrays, rotated, group_size, per_device, head_dim):
    tokens, width = arrays[0].shape
    count = len(arrays)
    step = tokens // 2
    scale = 1.0 / math.sqrt(head_dim)

    def kernel(*refs):
        out_ref, sign_ref = refs[-2:]

        @pl.when(pl.program_id(0) == 0)
        def _():
            sign_ref[...] = sign_block(head_dim)

        for index, ref in enumerate(refs[:-2]):
            for group in range(group_size):
                for head in range(per_device):
                    column = (group * per_device + head) * head_dim
                    block = ref[:, column : column + head_dim]
                    if rotated[index]:
                        turned = jnp.dot(block, sign_ref[...], preferred_element_type=jnp.float32)
                        block = (turned * scale).astype(jnp.bfloat16)
                    out_ref[group, index, head] = block

    return pl.pallas_call(
        kernel,
        grid=(tokens // step,),
        in_specs=[pl.BlockSpec((step, width), lambda g: (g, 0))] * count,
        out_specs=pl.BlockSpec(
            (group_size, count, per_device, step, head_dim), lambda g: (0, 0, 0, g, 0)
        ),
        out_shape=jax.ShapeDtypeStruct(
            (group_size, count, per_device, tokens, head_dim), jnp.bfloat16
        ),
        scratch_shapes=[pltpu.VMEM((head_dim, head_dim), jnp.bfloat16)],
        compiler_params=pltpu.CompilerParams(vmem_limit_bytes=VMEM_BYTES),
        cost_estimate=pl.CostEstimate(
            flops=2 * tokens * width * head_dim * sum(rotated),
            bytes_accessed=4 * tokens * width * count,
            transcendentals=0,
        ),
    )(*arrays)


def scores_of(query_now, keys_of, limit, first_active):
    scores = []
    largest = None
    for slot in range(0, len(keys_of), 2):
        keys_now = jnp.concatenate([keys_of[slot](), keys_of[slot + 1]()], axis=0)
        pair = lax.dot_general(
            query_now, keys_now, (((1,), (1,)), ((), ())), preferred_element_type=jnp.float32
        )
        half = pair.shape[1] // 2
        one, two = pair[:, :half], pair[:, half:]
        if slot >= first_active:
            one = jnp.where(limit > slot, one, -jnp.inf)
        two = jnp.where(limit > slot + 1, two, -jnp.inf)
        scores += [one, two]
        larger = jnp.maximum(one, two)
        largest = larger if largest is None else jnp.maximum(largest, larger)
    return scores, largest


def mix(scores, level, factor, values_of):
    total = None
    mixed = None
    for slot in range(0, len(scores), 2):
        one = jnp.exp2(scores[slot] * factor - level)
        two = jnp.exp2(scores[slot + 1] * factor - level)
        both = one + two
        total = both if total is None else total + both
        weights = jnp.concatenate([one.astype(jnp.bfloat16), two.astype(jnp.bfloat16)], axis=1)
        values_now = jnp.concatenate([values_of[slot](), values_of[slot + 1]()], axis=0)
        update = jnp.dot(weights, values_now, preferred_element_type=jnp.float32)
        mixed = update if mixed is None else mixed + update
    return jnp.sum(total, axis=1, keepdims=True), mixed


def tile_rows(ref, at, count, tile_len):
    at = jnp.clip(at, 0, count - 1)
    return lambda: ref[pl.ds(pl.multiple_of(at * tile_len, tile_len), tile_len), :]


def sort_lists(listed, counts, place, tiles_here, heads, reach):
    slots = listed.shape[1] // tiles_here

    def kernel(place_ref, listed_ref, counts_ref, inside_ref, halo_ref):
        first_head = place_ref[0]
        first_tile = place_ref[1]

        @pl.loop(0, heads)
        def _(head):
            @pl.loop(0, tiles_here)
            def _(tile):
                line = head * tiles_here + tile
                limit = counts_ref[first_head + head, tile]
                for spare in range(OWN_SLOTS):
                    inside_ref[line, spare] = 0
                for spare in range(HALO_SLOTS):
                    halo_ref[line, spare] = 0
                inside = jnp.int32(0)
                outside = jnp.int32(0)
                for slot in range(slots):
                    at = listed_ref[first_head + head, tile * slots + slot] - first_tile
                    is_inside = (at >= 0) & (at < tiles_here)
                    active = slot < limit

                    @pl.when(active & is_inside)
                    def _():
                        inside_ref[line, inside] = at

                    @pl.when(active & ~is_inside)
                    def _():
                        halo_ref[line, jnp.minimum(outside, HALO_SLOTS - 2)] = jnp.where(
                            at < 0, at + reach, at - tiles_here + reach
                        )

                    inside = inside + (active & is_inside).astype(jnp.int32)
                    outside = outside + (active & ~is_inside).astype(jnp.int32)
                inside_ref[line, OWN_SLOTS - 1] = inside
                halo_ref[line, HALO_SLOTS - 1] = outside

    smem = pl.BlockSpec(memory_space=pltpu.SMEM)
    lines = heads * tiles_here
    return pl.pallas_call(
        kernel,
        in_specs=[smem, smem, smem],
        out_specs=[smem, smem],
        out_shape=[
            jax.ShapeDtypeStruct((lines, OWN_SLOTS), jnp.int32),
            jax.ShapeDtypeStruct((lines, HALO_SLOTS), jnp.int32),
        ],
    )(place, listed, counts)


def tiles_of_step(step, tiles_here):
    last = tiles_here - 1
    return [2 * step, 2 * step + 1, last - 2 * step, last - 1 - 2 * step]


def most_of(limits):
    most = limits[0]
    for limit in limits[1:]:
        most = jnp.maximum(most, limit)
    return most


def attend_local(own, query, inside, tile_len):
    sources, _, heads, tokens, head_dim = own.shape
    rows = sources * tokens
    tiles_here = rows // tile_len
    slots = tiles_here
    factor = math.log2(math.e) / math.sqrt(head_dim)

    def kernel(inside_ref, own_ref, query_ref, mixed_ref, stats_ref, buf, sems):
        def copies(head):
            pairs = [(own_ref, 0), (own_ref, 1), (query_ref, 0)]
            return [
                pltpu.make_async_copy(
                    ref.at[:, index, head], buf.at[number, head], sems.at[head, number]
                )
                for number, (ref, index) in enumerate(pairs)
            ]

        for head in range(heads):
            for copy in copies(head):
                copy.start()

        @pl.loop(0, heads)
        def _(head):
            for copy in copies(head):
                copy.wait()
            key_rows, value_rows, query_rows = [
                buf.at[number, head].reshape(rows, head_dim) for number in range(3)
            ]
            column = pl.ds(pl.multiple_of(head * head_dim, head_dim), head_dim)

            @pl.loop(0, tiles_here // 4)
            def _(step):
                tiles = tiles_of_step(step, tiles_here)
                lines = [head * tiles_here + tile for tile in tiles]
                limits = [inside_ref[line, OWN_SLOTS - 1] for line in lines]
                most = most_of(limits)

                def work(used):
                    begun = []
                    for line, tile, limit in zip(lines, tiles, limits):
                        here = pl.ds(pl.multiple_of(tile * tile_len, tile_len), tile_len)
                        places = [inside_ref[line, slot] for slot in range(used)]
                        scores, largest = scores_of(
                            query_rows[here, :],
                            [tile_rows(key_rows, at, tiles_here, tile_len) for at in places],
                            limit,
                            1,
                        )
                        peak = jnp.max(largest, axis=1, keepdims=True) * factor
                        begun.append((here, places, scores, peak))
                    for here, places, scores, peak in begun:
                        total, mixed = mix(
                            scores,
                            peak,
                            factor,
                            [tile_rows(value_rows, at, tiles_here, tile_len) for at in places],
                        )
                        mixed_ref[here, column] = mixed / total
                        stats_ref[here, column] = jnp.broadcast_to(
                            peak + jnp.log2(total), (tile_len, head_dim)
                        )

                for used in range(2, slots + 1, 2):
                    @pl.when((most + 1) // 2 == used // 2)
                    def _():
                        work(used)

    smem = pl.BlockSpec(memory_space=pltpu.SMEM)
    hbm = pl.BlockSpec(memory_space=pl.ANY)
    vmem = pl.BlockSpec(memory_space=pltpu.VMEM)
    pairs = heads * tiles_here * slots
    state = jax.ShapeDtypeStruct((rows, heads * head_dim), jnp.float32)
    return pl.pallas_call(
        kernel,
        in_specs=[smem, hbm, hbm],
        out_specs=[vmem, vmem],
        out_shape=[state, state],
        scratch_shapes=[
            pltpu.VMEM((3, heads, sources, tokens, head_dim), jnp.bfloat16),
            pltpu.SemaphoreType.DMA((heads, 3)),
        ],
        compiler_params=pltpu.CompilerParams(vmem_limit_bytes=VMEM_BYTES // 3),
        cost_estimate=pl.CostEstimate(
            flops=4 * pairs * tile_len * tile_len * head_dim,
            bytes_accessed=2 * heads * head_dim * 7 * rows,
            transcendentals=pairs * tile_len * tile_len,
        ),
    )(inside, own, query)


def attend_halo(query, left, right, mixed, stats, halo, tile_len):
    sources, _, heads, tokens, head_dim = query.shape
    half = left.shape[0]
    rows = sources * tokens
    halo_rows = 2 * half * tokens
    halo_tiles = halo_rows // tile_len
    tiles_here = rows // tile_len
    factor = math.log2(math.e) / math.sqrt(head_dim)

    def kernel(halo_ref, query_ref, left_ref, right_ref, mixed_ref, stats_ref, out_ref,
               buf, query_buf, sems):
        def copies(head):
            pairs = [(query_ref.at[:, 0, head], query_buf.at[head])]
            for index in range(2):
                pairs.append((left_ref.at[:, index, head], buf.at[index, head, pl.ds(0, half)]))
                pairs.append((right_ref.at[:, index, head], buf.at[index, head, pl.ds(half, half)]))
            return [
                pltpu.make_async_copy(there, here, sems.at[head, number])
                for number, (there, here) in enumerate(pairs)
            ]

        for head in range(heads):
            for copy in copies(head):
                copy.start()

        @pl.loop(0, heads)
        def _(head):
            for copy in copies(head):
                copy.wait()
            key_rows, value_rows = [
                buf.at[index, head].reshape(halo_rows, head_dim) for index in range(2)
            ]
            query_rows = query_buf.at[head].reshape(rows, head_dim)
            column = pl.ds(pl.multiple_of(head * head_dim, head_dim), head_dim)

            @pl.loop(0, tiles_here // 4)
            def _(step):
                tiles = tiles_of_step(step, tiles_here)
                lines = [head * tiles_here + tile for tile in tiles]
                limits = [halo_ref[line, HALO_SLOTS - 1] for line in lines]
                most = most_of(limits)

                def work(used):
                    begun = []
                    for line, tile, limit in zip(lines, tiles, limits):
                        here = pl.ds(pl.multiple_of(tile * tile_len, tile_len), tile_len)
                        if not used:
                            out_ref[here, column] = mixed_ref[here, column].astype(jnp.bfloat16)
                            continue
                        places = [halo_ref[line, slot] for slot in range(used)]
                        scores, largest = scores_of(
                            query_rows[here, :],
                            [tile_rows(key_rows, at, halo_tiles, tile_len) for at in places],
                            limit,
                            0,
                        )
                        level = stats_ref[here, column]
                        newest = jnp.maximum(level, jnp.max(largest, axis=1, keepdims=True) * factor)
                        begun.append((here, places, scores, newest, jnp.exp2(level - newest)))
                    for here, places, scores, newest, fade in begun:
                        added, update = mix(
                            scores,
                            newest,
                            factor,
                            [tile_rows(value_rows, at, halo_tiles, tile_len) for at in places],
                        )
                        out_ref[here, column] = (
                            (mixed_ref[here, column] * fade + update) / (fade + added)
                        ).astype(jnp.bfloat16)

                for used in range(0, HALO_SLOTS - 1, 2):
                    @pl.when((most + 1) // 2 == used // 2)
                    def _():
                        work(used)

    smem = pl.BlockSpec(memory_space=pltpu.SMEM)
    hbm = pl.BlockSpec(memory_space=pl.ANY)
    vmem = pl.BlockSpec(memory_space=pltpu.VMEM)
    pairs = heads * tiles_here * (HALO_SLOTS - 2) // 2
    return pl.pallas_call(
        kernel,
        in_specs=[smem, hbm, hbm, hbm, vmem, vmem],
        out_specs=vmem,
        out_shape=jax.ShapeDtypeStruct((rows, heads * head_dim), jnp.bfloat16),
        scratch_shapes=[
            pltpu.VMEM((2, heads, 2 * half, tokens, head_dim), jnp.bfloat16),
            pltpu.VMEM((heads, sources, tokens, head_dim), jnp.bfloat16),
            pltpu.SemaphoreType.DMA((heads, 5)),
        ],
        compiler_params=pltpu.CompilerParams(vmem_limit_bytes=VMEM_BYTES // 3),
        cost_estimate=pl.CostEstimate(
            flops=4 * pairs * tile_len * tile_len * head_dim,
            bytes_accessed=2 * heads * head_dim * (2 * halo_rows + 6 * rows),
            transcendentals=pairs * tile_len * tile_len,
        ),
    )(halo, query, left, right, mixed, stats)


def body(queries, keys, values, neighbours, counts):
    group_size = lax.axis_size("head")
    blocks = lax.axis_size("seq")
    local_tokens, feature_width = queries.shape
    head_count, tiles_here = counts.shape
    head_dim = feature_width // head_count
    per_device = head_count // group_size
    tile_len = local_tokens * group_size // tiles_here
    half = group_size // 2
    halo_tiles = half * local_tokens // tile_len

    def exchange(array):
        return lax.all_to_all(array, "head", split_axis=0, concat_axis=0, tiled=True)

    own = exchange(prepare([keys, values], [True, False], group_size, per_device, head_dim))
    query = exchange(prepare([queries], [True], group_size, per_device, head_dim))
    place = jnp.stack(
        [lax.axis_index("head") * per_device, lax.axis_index("seq") * tiles_here]
    ).astype(jnp.int32)
    listed = neighbours.reshape(head_count, -1)
    inside, halo = sort_lists(listed, counts, place, tiles_here, per_device, halo_tiles)
    up = [(i, i + 1) for i in range(blocks - 1)]
    down = [(i + 1, i) for i in range(blocks - 1)]
    left = lax.ppermute(own[group_size - half :], "seq", up)
    right = lax.ppermute(own[:half], "seq", down)
    mixed, stats = attend_local(own, query, inside, tile_len)
    result = attend_halo(query, left, right, mixed, stats, halo, tile_len)
    result = exchange(result.reshape(group_size, local_tokens, per_device * head_dim))
    return jnp.moveaxis(result, 0, 1).reshape(local_tokens, feature_width)


def solution(mesh):
    placed = (
        P(("seq", "head"), None),
        P(("seq", "head"), None),
        P(("seq", "head"), None),
        P(None, "seq", None),
        P(None, "seq"),
    )
    return jax.shard_map(
        body, mesh=mesh, in_specs=placed, out_specs=P(("seq", "head"), None), check_vma=False
    )
```

```python
import math

import jax
import jax.numpy as jnp
from jax import lax
from jax.experimental import pallas as pl
from jax.experimental.pallas import tpu as pltpu
from jax.sharding import PartitionSpec as P

VMEM_BYTES = 60 * 1024 * 1024
ROW = 4
OWN_SLOTS = 16
HALO_SLOTS = 8


def sign_block(size):
    row = lax.broadcasted_iota(jnp.int32, (size, size), 0)
    column = lax.broadcasted_iota(jnp.int32, (size, size), 1)
    common = jnp.bitwise_and(row, column)
    parity = jnp.zeros((size, size), jnp.int32)
    for bit_level in range(max(size.bit_length() - 1, 1)):
        parity = parity + jnp.bitwise_and(jnp.right_shift(common, bit_level), 1)
    return (1 - 2 * jnp.bitwise_and(parity, 1)).astype(jnp.float32).astype(jnp.bfloat16)


def odd_row(block):
    return (block // ROW) % 2


def owner_block(member, odd, group_size):
    return ((member // 2 + (member % 2) * odd) % (group_size // 2)) * 2 + member % 2


def owner_of(block, head_block, group_size):
    shift = (head_block % 2) * odd_row(block)
    return ((head_block // 2 - shift) % (group_size // 2)) * 2 + head_block % 2


def prepare(arrays, rotated, group_size, per_device, head_dim):
    tokens, width = arrays[0].shape
    count = len(arrays)
    step = tokens // 2
    scale = 1.0 / math.sqrt(head_dim)

    def kernel(*refs):
        out_ref, sign_ref = refs[-2:]

        @pl.when(pl.program_id(0) == 0)
        def _():
            sign_ref[...] = sign_block(head_dim)

        odd = odd_row(lax.axis_index("seq"))
        for index, ref in enumerate(refs[:-2]):
            for group in range(group_size):
                first = owner_block(group, odd, group_size) * per_device
                for head in range(per_device):
                    column = pl.multiple_of((first + head) * head_dim, head_dim)
                    block = ref[:, pl.ds(column, head_dim)]
                    if rotated[index]:
                        turned = jnp.dot(block, sign_ref[...], preferred_element_type=jnp.float32)
                        block = (turned * scale).astype(jnp.bfloat16)
                    out_ref[group, index, head] = block

    return pl.pallas_call(
        kernel,
        grid=(tokens // step,),
        in_specs=[pl.BlockSpec((step, width), lambda g: (g, 0))] * count,
        out_specs=pl.BlockSpec(
            (group_size, count, per_device, step, head_dim), lambda g: (0, 0, 0, g, 0)
        ),
        out_shape=jax.ShapeDtypeStruct(
            (group_size, count, per_device, tokens, head_dim), jnp.bfloat16
        ),
        scratch_shapes=[pltpu.VMEM((head_dim, head_dim), jnp.bfloat16)],
        compiler_params=pltpu.CompilerParams(vmem_limit_bytes=VMEM_BYTES),
        cost_estimate=pl.CostEstimate(
            flops=2 * tokens * width * head_dim * sum(rotated),
            bytes_accessed=4 * tokens * width * count,
            transcendentals=0,
        ),
    )(*arrays)


def scores_of(query_now, keys_of, limit, first_active):
    scores = []
    largest = None
    for slot in range(0, len(keys_of), 2):
        keys_now = jnp.concatenate([keys_of[slot](), keys_of[slot + 1]()], axis=0)
        pair = lax.dot_general(
            query_now, keys_now, (((1,), (1,)), ((), ())), preferred_element_type=jnp.float32
        )
        half = pair.shape[1] // 2
        one, two = pair[:, :half], pair[:, half:]
        if slot >= first_active:
            one = jnp.where(limit > slot, one, -jnp.inf)
        two = jnp.where(limit > slot + 1, two, -jnp.inf)
        scores += [one, two]
        larger = jnp.maximum(one, two)
        largest = larger if largest is None else jnp.maximum(largest, larger)
    return scores, largest


def mix(scores, level, factor, values_of):
    total = None
    mixed = None
    for slot in range(0, len(scores), 2):
        one = jnp.exp2(scores[slot] * factor - level)
        two = jnp.exp2(scores[slot + 1] * factor - level)
        both = one + two
        total = both if total is None else total + both
        weights = jnp.concatenate([one.astype(jnp.bfloat16), two.astype(jnp.bfloat16)], axis=1)
        values_now = jnp.concatenate([values_of[slot](), values_of[slot + 1]()], axis=0)
        update = jnp.dot(weights, values_now, preferred_element_type=jnp.float32)
        mixed = update if mixed is None else mixed + update
    return jnp.sum(total, axis=1, keepdims=True), mixed


def tile_rows(ref, at, count, tile_len):
    at = jnp.clip(at, 0, count - 1)
    return lambda: ref[pl.ds(pl.multiple_of(at * tile_len, tile_len), tile_len), :]


def sort_lists(listed, counts, place, tiles_here, heads, reach):
    slots = listed.shape[1] // tiles_here

    def kernel(place_ref, listed_ref, counts_ref, inside_ref, halo_ref):
        first_head = place_ref[0]
        first_tile = place_ref[1]

        @pl.loop(0, heads)
        def _(head):
            @pl.loop(0, tiles_here)
            def _(tile):
                line = head * tiles_here + tile
                limit = counts_ref[first_head + head, tile]
                for spare in range(OWN_SLOTS):
                    inside_ref[line, spare] = 0
                for spare in range(HALO_SLOTS):
                    halo_ref[line, spare] = 0
                inside = jnp.int32(0)
                outside = jnp.int32(0)
                for slot in range(slots):
                    at = listed_ref[first_head + head, tile * slots + slot] - first_tile
                    is_inside = (at >= 0) & (at < tiles_here)
                    active = slot < limit

                    @pl.when(active & is_inside)
                    def _():
                        inside_ref[line, inside] = at

                    @pl.when(active & ~is_inside)
                    def _():
                        halo_ref[line, jnp.minimum(outside, HALO_SLOTS - 2)] = jnp.where(
                            at < 0, at + reach, at - tiles_here + reach
                        )

                    inside = inside + (active & is_inside).astype(jnp.int32)
                    outside = outside + (active & ~is_inside).astype(jnp.int32)
                inside_ref[line, OWN_SLOTS - 1] = inside
                halo_ref[line, HALO_SLOTS - 1] = outside

    smem = pl.BlockSpec(memory_space=pltpu.SMEM)
    lines = heads * tiles_here
    return pl.pallas_call(
        kernel,
        in_specs=[smem, smem, smem],
        out_specs=[smem, smem],
        out_shape=[
            jax.ShapeDtypeStruct((lines, OWN_SLOTS), jnp.int32),
            jax.ShapeDtypeStruct((lines, HALO_SLOTS), jnp.int32),
        ],
    )(place, listed, counts)


def tiles_of_step(step, tiles_here):
    last = tiles_here - 1
    return [2 * step, 2 * step + 1, last - 2 * step, last - 1 - 2 * step]


def most_of(limits):
    most = limits[0]
    for limit in limits[1:]:
        most = jnp.maximum(most, limit)
    return most


def attend_local(own, query, inside, tile_len):
    sources, _, heads, tokens, head_dim = own.shape
    rows = sources * tokens
    tiles_here = rows // tile_len
    slots = tiles_here
    factor = math.log2(math.e) / math.sqrt(head_dim)

    def kernel(inside_ref, own_ref, query_ref, mixed_ref, stats_ref, buf, sems):
        def copies(head):
            pairs = [(own_ref, 0), (own_ref, 1), (query_ref, 0)]
            return [
                pltpu.make_async_copy(
                    ref.at[:, index, head], buf.at[number, head], sems.at[head, number]
                )
                for number, (ref, index) in enumerate(pairs)
            ]

        for head in range(heads):
            for copy in copies(head):
                copy.start()

        @pl.loop(0, heads)
        def _(head):
            for copy in copies(head):
                copy.wait()
            key_rows, value_rows, query_rows = [
                buf.at[number, head].reshape(rows, head_dim) for number in range(3)
            ]
            column = pl.ds(pl.multiple_of(head * head_dim, head_dim), head_dim)

            @pl.loop(0, tiles_here // 4)
            def _(step):
                tiles = tiles_of_step(step, tiles_here)
                lines = [head * tiles_here + tile for tile in tiles]
                limits = [inside_ref[line, OWN_SLOTS - 1] for line in lines]
                most = most_of(limits)

                def work(used):
                    begun = []
                    for line, tile, limit in zip(lines, tiles, limits):
                        here = pl.ds(pl.multiple_of(tile * tile_len, tile_len), tile_len)
                        places = [inside_ref[line, slot] for slot in range(used)]
                        scores, largest = scores_of(
                            query_rows[here, :],
                            [tile_rows(key_rows, at, tiles_here, tile_len) for at in places],
                            limit,
                            1,
                        )
                        peak = jnp.max(largest, axis=1, keepdims=True) * factor
                        begun.append((here, places, scores, peak))
                    for here, places, scores, peak in begun:
                        total, mixed = mix(
                            scores,
                            peak,
                            factor,
                            [tile_rows(value_rows, at, tiles_here, tile_len) for at in places],
                        )
                        mixed_ref[here, column] = mixed / total
                        stats_ref[here, column] = jnp.broadcast_to(
                            peak + jnp.log2(total), (tile_len, head_dim)
                        )

                for used in range(2, slots + 1, 2):
                    @pl.when((most + 1) // 2 == used // 2)
                    def _():
                        work(used)

    smem = pl.BlockSpec(memory_space=pltpu.SMEM)
    hbm = pl.BlockSpec(memory_space=pl.ANY)
    vmem = pl.BlockSpec(memory_space=pltpu.VMEM)
    pairs = heads * tiles_here * slots
    state = jax.ShapeDtypeStruct((rows, heads * head_dim), jnp.float32)
    return pl.pallas_call(
        kernel,
        in_specs=[smem, hbm, hbm],
        out_specs=[vmem, vmem],
        out_shape=[state, state],
        scratch_shapes=[
            pltpu.VMEM((3, heads, sources, tokens, head_dim), jnp.bfloat16),
            pltpu.SemaphoreType.DMA((heads, 3)),
        ],
        compiler_params=pltpu.CompilerParams(vmem_limit_bytes=VMEM_BYTES // 3),
        cost_estimate=pl.CostEstimate(
            flops=4 * pairs * tile_len * tile_len * head_dim,
            bytes_accessed=2 * heads * head_dim * 7 * rows,
            transcendentals=pairs * tile_len * tile_len,
        ),
    )(inside, own, query)


def attend_halo(query, left, right, crossed, mixed, stats, halo, ends, tile_len):
    sources, _, heads, tokens, head_dim = query.shape
    half = left[0].shape[0]
    rows = sources * tokens
    halo_rows = 2 * half * tokens
    halo_tiles = halo_rows // tile_len
    reach = halo_tiles // 2
    tiles_here = rows // tile_len
    factor = math.log2(math.e) / math.sqrt(head_dim)
    needs = [max(reach - tile, tile - tiles_here + 1 + reach) for tile in range(tiles_here)]

    def kernel(halo_ref, ends_ref, query_ref, left_k, left_v, right_k, right_v, crossed_k, crossed_v,
               mixed_ref, stats_ref, out_ref, buf, query_buf, sems):
        def query_copy(head):
            return pltpu.make_async_copy(
                query_ref.at[:, 0, head], query_buf.at[head], sems.at[head, 0]
            )

        def side_copy(head, index, side, ref):
            return pltpu.make_async_copy(
                ref.at[:, head],
                buf.at[index, head, pl.ds(side * half, half)],
                sems.at[head, 1 + 2 * index + side],
            )

        sides = [
            (0, 0, left_k, crossed_k),
            (0, 1, right_k, crossed_k),
            (1, 0, left_v, crossed_v),
            (1, 1, right_v, crossed_v),
        ]
        for head in range(heads):
            query_copy(head).start()
            for index, side, straight, other in sides:
                is_other = ends_ref[side] == 1

                @pl.when(is_other)
                def _():
                    side_copy(head, index, side, other).start()

                @pl.when(jnp.logical_not(is_other))
                def _():
                    side_copy(head, index, side, straight).start()

        @pl.loop(0, heads)
        def _(head):
            query_copy(head).wait()
            for index, side, straight, _ in sides:
                side_copy(head, index, side, straight).wait()
            key_rows, value_rows = [
                buf.at[index, head].reshape(halo_rows, head_dim) for index in range(2)
            ]
            query_rows = query_buf.at[head].reshape(rows, head_dim)
            column = pl.ds(pl.multiple_of(head * head_dim, head_dim), head_dim)
            lines = [head * tiles_here + tile for tile in range(tiles_here)]
            limits = [halo_ref[line, HALO_SLOTS - 1] for line in lines]
            most = most_of(limits)

            def work(cap):
                begun = []
                for tile in range(tiles_here):
                    here = slice(tile * tile_len, (tile + 1) * tile_len)
                    used = min(cap, needs[tile] + needs[tile] % 2)
                    if not used:
                        out_ref[here, column] = mixed_ref[here, column].astype(jnp.bfloat16)
                        continue
                    places = [halo_ref[lines[tile], slot] for slot in range(used)]
                    scores, largest = scores_of(
                        query_rows[here, :],
                        [tile_rows(key_rows, at, halo_tiles, tile_len) for at in places],
                        limits[tile],
                        0,
                    )
                    level = stats_ref[here, column]
                    newest = jnp.maximum(level, jnp.max(largest, axis=1, keepdims=True) * factor)
                    begun.append((here, places, scores, newest, jnp.exp2(level - newest)))
                for here, places, scores, newest, fade in begun:
                    added, update = mix(
                        scores,
                        newest,
                        factor,
                        [tile_rows(value_rows, at, halo_tiles, tile_len) for at in places],
                    )
                    out_ref[here, column] = (
                        (mixed_ref[here, column] * fade + update) / (fade + added)
                    ).astype(jnp.bfloat16)

            for cap in range(0, HALO_SLOTS - 1, 2):
                @pl.when((most + 1) // 2 == cap // 2)
                def _():
                    work(cap)

    smem = pl.BlockSpec(memory_space=pltpu.SMEM)
    hbm = pl.BlockSpec(memory_space=pl.ANY)
    vmem = pl.BlockSpec(memory_space=pltpu.VMEM)
    pairs = heads * tiles_here * (HALO_SLOTS - 2) // 2
    return pl.pallas_call(
        kernel,
        in_specs=[smem, smem] + [hbm] * 7 + [vmem, vmem],
        out_specs=vmem,
        out_shape=jax.ShapeDtypeStruct((rows, heads * head_dim), jnp.bfloat16),
        scratch_shapes=[
            pltpu.VMEM((2, heads, 2 * half, tokens, head_dim), jnp.bfloat16),
            pltpu.VMEM((heads, sources, tokens, head_dim), jnp.bfloat16),
            pltpu.SemaphoreType.DMA((heads, 5)),
        ],
        compiler_params=pltpu.CompilerParams(vmem_limit_bytes=VMEM_BYTES // 3),
        cost_estimate=pl.CostEstimate(
            flops=4 * pairs * tile_len * tile_len * head_dim,
            bytes_accessed=2 * heads * head_dim * (2 * halo_rows + 6 * rows),
            transcendentals=pairs * tile_len * tile_len,
        ),
    )(halo, ends, query, *left, *right, *crossed, mixed, stats)


def routes(blocks, group_size):
    on = []
    across = []
    for block in range(blocks):
        there = block + 1
        if there % ROW == 0:
            there = block + 1 - ROW if odd_row(block) == 0 else block + 1 + ROW
        if there < blocks:
            on += [(block * group_size + m, there * group_size + m) for m in range(group_size)]
        if block % ROW in (0, ROW - 1):
            other = block + ROW if odd_row(block) == 0 else block - ROW
            across += [
                tuple(at * group_size + owner_of(at, head_block, group_size) for at in (block, other))
                for head_block in range(group_size)
            ]
    back = []
    for block in range(blocks):
        there = block - 1
        if block % ROW == 0:
            there = block - 1 + ROW if odd_row(block) == 1 else block - 1 - ROW
        if there >= 0:
            back += [(block * group_size + m, there * group_size + m) for m in range(group_size)]
    return on, back, across


def assemble(parts):
    members, tokens, width = parts.shape
    step = tokens // 2

    def kernel(parts_ref, out_ref):
        odd = odd_row(lax.axis_index("seq"))
        for member in range(members):
            column = pl.multiple_of(owner_block(member, odd, members) * width, width)
            out_ref[:, pl.ds(column, width)] = parts_ref[member]

    return pl.pallas_call(
        kernel,
        grid=(tokens // step,),
        in_specs=[pl.BlockSpec((members, step, width), lambda g: (0, g, 0))],
        out_specs=pl.BlockSpec((step, members * width), lambda g: (g, 0)),
        out_shape=jax.ShapeDtypeStruct((tokens, members * width), parts.dtype),
        compiler_params=pltpu.CompilerParams(vmem_limit_bytes=VMEM_BYTES),
        cost_estimate=pl.CostEstimate(
            flops=0, bytes_accessed=4 * tokens * members * width, transcendentals=0
        ),
    )(parts)


def body(queries, keys, values, neighbours, counts):
    group_size = lax.axis_size("head")
    blocks = lax.axis_size("seq")
    local_tokens, feature_width = queries.shape
    head_count, tiles_here = counts.shape
    head_dim = feature_width // head_count
    per_device = head_count // group_size
    tile_len = local_tokens * group_size // tiles_here
    half = group_size // 2
    halo_tiles = half * local_tokens // tile_len

    def exchange(array):
        return lax.all_to_all(array, "head", split_axis=0, concat_axis=0, tiled=True)

    own = exchange(prepare([keys, values], [True, False], group_size, per_device, head_dim))
    query = exchange(prepare([queries], [True], group_size, per_device, head_dim))
    block = lax.axis_index("seq")
    head_block = owner_block(lax.axis_index("head"), odd_row(block), group_size)
    place = jnp.stack([head_block * per_device, block * tiles_here]).astype(jnp.int32)
    at_start = block % ROW == 0
    ends = jnp.stack([at_start, block % ROW == ROW - 1]).astype(jnp.int32)
    listed = neighbours.reshape(head_count, -1)
    inside, halo = sort_lists(listed, counts, place, tiles_here, per_device, halo_tiles)
    on, back, across = routes(blocks, group_size)
    both = ("seq", "head")
    left = [lax.ppermute(own[group_size - half :, index], both, on) for index in range(2)]
    right = [lax.ppermute(own[:half, index], both, back) for index in range(2)]
    crossed = [
        lax.ppermute(jnp.where(at_start, one, two), both, across) for one, two in zip(left, right)
    ]
    mixed, stats = attend_local(own, query, inside, tile_len)
    result = attend_halo(query, left, right, crossed, mixed, stats, halo, ends, tile_len)
    result = exchange(result.reshape(group_size, local_tokens, per_device * head_dim))
    return assemble(result)


def solution(mesh):
    placed = (
        P(("seq", "head"), None),
        P(("seq", "head"), None),
        P(("seq", "head"), None),
        P(None, "seq", None),
        P(None, "seq"),
    )
    return jax.shard_map(
        body, mesh=mesh, in_specs=placed, out_specs=P(("seq", "head"), None), check_vma=False
    )
```

```python
import math

import jax
import jax.numpy as jnp
from jax import lax
from jax.experimental import pallas as pl
from jax.experimental.pallas import tpu as pltpu
from jax.sharding import PartitionSpec as P

VMEM_BYTES = 60 * 1024 * 1024
ROW = 4
OWN_SLOTS = 16
INNER, OUTER, CROSSED = range(3)
HALO_SLOTS = 8


def sign_block(size):
    row = lax.broadcasted_iota(jnp.int32, (size, size), 0)
    column = lax.broadcasted_iota(jnp.int32, (size, size), 1)
    common = jnp.bitwise_and(row, column)
    parity = jnp.zeros((size, size), jnp.int32)
    for bit_level in range(max(size.bit_length() - 1, 1)):
        parity = parity + jnp.bitwise_and(jnp.right_shift(common, bit_level), 1)
    return (1 - 2 * jnp.bitwise_and(parity, 1)).astype(jnp.float32).astype(jnp.bfloat16)


def odd_row(block):
    return (block // ROW) % 2


def owner_block(member, odd, group_size):
    return ((member // 2 + (member % 2) * odd) % (group_size // 2)) * 2 + member % 2


def owner_of(block, head_block, group_size):
    shift = (head_block % 2) * odd_row(block)
    return ((head_block // 2 - shift) % (group_size // 2)) * 2 + head_block % 2


def prepare(arrays, rotated, group_size, per_device, head_dim):
    tokens, width = arrays[0].shape
    count = len(arrays)
    step = tokens // 2
    scale = 1.0 / math.sqrt(head_dim)

    def kernel(*refs):
        out_ref, sign_ref = refs[-2:]

        @pl.when(pl.program_id(0) == 0)
        def _():
            sign_ref[...] = sign_block(head_dim)

        odd = odd_row(lax.axis_index("seq"))
        for index, ref in enumerate(refs[:-2]):
            for group in range(group_size):
                first = owner_block(group, odd, group_size) * per_device
                for head in range(per_device):
                    column = pl.multiple_of((first + head) * head_dim, head_dim)
                    block = ref[:, pl.ds(column, head_dim)]
                    if rotated[index]:
                        turned = jnp.dot(block, sign_ref[...], preferred_element_type=jnp.float32)
                        block = (turned * scale).astype(jnp.bfloat16)
                    out_ref[group, index, head] = block

    return pl.pallas_call(
        kernel,
        grid=(tokens // step,),
        in_specs=[pl.BlockSpec((step, width), lambda g: (g, 0))] * count,
        out_specs=pl.BlockSpec(
            (group_size, count, per_device, step, head_dim), lambda g: (0, 0, 0, g, 0)
        ),
        out_shape=jax.ShapeDtypeStruct(
            (group_size, count, per_device, tokens, head_dim), jnp.bfloat16
        ),
        scratch_shapes=[pltpu.VMEM((head_dim, head_dim), jnp.bfloat16)],
        compiler_params=pltpu.CompilerParams(vmem_limit_bytes=VMEM_BYTES),
        cost_estimate=pl.CostEstimate(
            flops=2 * tokens * width * head_dim * sum(rotated),
            bytes_accessed=4 * tokens * width * count,
            transcendentals=0,
        ),
    )(*arrays)


def scores_of(query_now, keys_of, limit, first_active):
    scores = []
    largest = None
    for slot in range(0, len(keys_of), 2):
        keys_now = jnp.concatenate([keys_of[slot](), keys_of[slot + 1]()], axis=0)
        pair = lax.dot_general(
            query_now, keys_now, (((1,), (1,)), ((), ())), preferred_element_type=jnp.float32
        )
        half = pair.shape[1] // 2
        one, two = pair[:, :half], pair[:, half:]
        if slot >= first_active:
            one = jnp.where(limit > slot, one, -jnp.inf)
        two = jnp.where(limit > slot + 1, two, -jnp.inf)
        scores += [one, two]
        larger = jnp.maximum(one, two)
        largest = larger if largest is None else jnp.maximum(largest, larger)
    return scores, largest


def mix(scores, level, factor, values_of):
    total = None
    mixed = None
    for slot in range(0, len(scores), 2):
        one = jnp.exp2(scores[slot] * factor - level)
        two = jnp.exp2(scores[slot + 1] * factor - level)
        both = one + two
        total = both if total is None else total + both
        weights = jnp.concatenate([one.astype(jnp.bfloat16), two.astype(jnp.bfloat16)], axis=1)
        values_now = jnp.concatenate([values_of[slot](), values_of[slot + 1]()], axis=0)
        update = jnp.dot(weights, values_now, preferred_element_type=jnp.float32)
        mixed = update if mixed is None else mixed + update
    return jnp.sum(total, axis=1, keepdims=True), mixed


def tile_rows(ref, at, count, tile_len):
    at = jnp.clip(at, 0, count - 1)
    return lambda: ref[pl.ds(pl.multiple_of(at * tile_len, tile_len), tile_len), :]


def sort_lists(listed, counts, place, tiles_here, heads, reach):
    slots = listed.shape[1] // tiles_here

    def kernel(place_ref, listed_ref, counts_ref, inside_ref, halo_ref):
        first_head = place_ref[0]
        first_tile = place_ref[1]

        @pl.loop(0, heads)
        def _(head):
            @pl.loop(0, tiles_here)
            def _(tile):
                line = head * tiles_here + tile
                limit = counts_ref[first_head + head, tile]
                for spare in range(OWN_SLOTS):
                    inside_ref[line, spare] = 0
                for spare in range(HALO_SLOTS):
                    halo_ref[line, spare] = 0
                inside = jnp.int32(0)
                outside = jnp.int32(0)
                for slot in range(slots):
                    at = listed_ref[first_head + head, tile * slots + slot] - first_tile
                    is_inside = (at >= 0) & (at < tiles_here)
                    active = slot < limit

                    @pl.when(active & is_inside)
                    def _():
                        inside_ref[line, inside] = at

                    @pl.when(active & ~is_inside)
                    def _():
                        halo_ref[line, jnp.minimum(outside, HALO_SLOTS - 2)] = jnp.where(
                            at < 0, at + reach, at - tiles_here + reach
                        )

                    inside = inside + (active & is_inside).astype(jnp.int32)
                    outside = outside + (active & ~is_inside).astype(jnp.int32)
                inside_ref[line, OWN_SLOTS - 1] = inside
                halo_ref[line, HALO_SLOTS - 1] = outside

    smem = pl.BlockSpec(memory_space=pltpu.SMEM)
    lines = heads * tiles_here
    return pl.pallas_call(
        kernel,
        in_specs=[smem, smem, smem],
        out_specs=[smem, smem],
        out_shape=[
            jax.ShapeDtypeStruct((lines, OWN_SLOTS), jnp.int32),
            jax.ShapeDtypeStruct((lines, HALO_SLOTS), jnp.int32),
        ],
    )(place, listed, counts)


def tiles_of_step(step, tiles_here):
    last = tiles_here - 1
    return [2 * step, 2 * step + 1, last - 2 * step, last - 1 - 2 * step]


def most_of(limits):
    most = limits[0]
    for limit in limits[1:]:
        most = jnp.maximum(most, limit)
    return most


def attend_local(own, query, inside, tile_len):
    sources, _, heads, tokens, head_dim = own.shape
    rows = sources * tokens
    tiles_here = rows // tile_len
    slots = tiles_here
    factor = math.log2(math.e) / math.sqrt(head_dim)

    def kernel(inside_ref, own_ref, query_ref, mixed_ref, stats_ref, buf, sems):
        def copies(head):
            pairs = [(own_ref, 0), (own_ref, 1), (query_ref, 0)]
            return [
                pltpu.make_async_copy(
                    ref.at[:, index, head], buf.at[number, head], sems.at[head, number]
                )
                for number, (ref, index) in enumerate(pairs)
            ]

        for head in range(heads):
            for copy in copies(head):
                copy.start()

        @pl.loop(0, heads)
        def _(head):
            for copy in copies(head):
                copy.wait()
            key_rows, value_rows, query_rows = [
                buf.at[number, head].reshape(rows, head_dim) for number in range(3)
            ]
            column = pl.ds(pl.multiple_of(head * head_dim, head_dim), head_dim)

            @pl.loop(0, tiles_here // 4)
            def _(step):
                tiles = tiles_of_step(step, tiles_here)
                lines = [head * tiles_here + tile for tile in tiles]
                limits = [inside_ref[line, OWN_SLOTS - 1] for line in lines]
                most = most_of(limits)

                def work(used):
                    begun = []
                    for line, tile, limit in zip(lines, tiles, limits):
                        here = pl.ds(pl.multiple_of(tile * tile_len, tile_len), tile_len)
                        places = [inside_ref[line, slot] for slot in range(used)]
                        scores, largest = scores_of(
                            query_rows[here, :],
                            [tile_rows(key_rows, at, tiles_here, tile_len) for at in places],
                            limit,
                            1,
                        )
                        peak = jnp.max(largest, axis=1, keepdims=True) * factor
                        begun.append((here, places, scores, peak))
                    for here, places, scores, peak in begun:
                        total, mixed = mix(
                            scores,
                            peak,
                            factor,
                            [tile_rows(value_rows, at, tiles_here, tile_len) for at in places],
                        )
                        mixed_ref[here, column] = mixed / total
                        stats_ref[here, column] = jnp.broadcast_to(
                            peak + jnp.log2(total), (tile_len, head_dim)
                        )

                for used in range(2, slots + 1, 2):
                    @pl.when((most + 1) // 2 == used // 2)
                    def _():
                        work(used)

    smem = pl.BlockSpec(memory_space=pltpu.SMEM)
    hbm = pl.BlockSpec(memory_space=pl.ANY)
    vmem = pl.BlockSpec(memory_space=pltpu.VMEM)
    pairs = heads * tiles_here * slots
    state = jax.ShapeDtypeStruct((rows, heads * head_dim), jnp.float32)
    return pl.pallas_call(
        kernel,
        in_specs=[smem, hbm, hbm],
        out_specs=[vmem, vmem],
        out_shape=[state, state],
        scratch_shapes=[
            pltpu.VMEM((3, heads, sources, tokens, head_dim), jnp.bfloat16),
            pltpu.SemaphoreType.DMA((heads, 3)),
        ],
        compiler_params=pltpu.CompilerParams(vmem_limit_bytes=VMEM_BYTES // 3),
        cost_estimate=pl.CostEstimate(
            flops=4 * pairs * tile_len * tile_len * head_dim,
            bytes_accessed=2 * heads * head_dim * 7 * rows,
            transcendentals=pairs * tile_len * tile_len,
        ),
    )(inside, own, query)


def attend_halo(query, outer, inner, crossed, mixed, stats, halo, kinds, tile_len):
    sources, _, heads, tokens, head_dim = query.shape
    half = inner.shape[0]
    rows = sources * tokens
    halo_rows = 2 * half * tokens
    halo_tiles = halo_rows // tile_len
    reach = halo_tiles // 2
    tiles_here = rows // tile_len
    factor = math.log2(math.e) / math.sqrt(head_dim)
    needs = [max(reach - tile, tile - tiles_here + 1 + reach) for tile in range(tiles_here)]

    def kernel(halo_ref, kinds_ref, query_ref, outer_k, outer_v, crossed_k, crossed_v, inner_ref,
               mixed_ref, stats_ref, out_ref, buf, query_buf, sems):
        def query_copy(head):
            return pltpu.make_async_copy(
                query_ref.at[:, 0, head], query_buf.at[head], sems.at[head, 0]
            )

        def side_copy(head, index, side, kind):
            if kind == INNER:
                source = inner_ref.at[:, index, head]
            elif kind == OUTER:
                source = (outer_k, outer_v)[index].at[:, head]
            else:
                source = (crossed_k, crossed_v)[index].at[:, head]
            return pltpu.make_async_copy(
                source,
                buf.at[index, head, pl.ds(side * half, half)],
                sems.at[head, 1 + 2 * index + side],
            )

        for head in range(heads):
            query_copy(head).start()
            for side in range(2):
                for kind in (INNER, OUTER, CROSSED):
                    @pl.when(kinds_ref[side] == kind)
                    def _():
                        for index in range(2):
                            side_copy(head, index, side, kind).start()

        @pl.loop(0, heads)
        def _(head):
            query_copy(head).wait()
            for side in range(2):
                for index in range(2):
                    side_copy(head, index, side, INNER).wait()
            key_rows, value_rows = [
                buf.at[index, head].reshape(halo_rows, head_dim) for index in range(2)
            ]
            query_rows = query_buf.at[head].reshape(rows, head_dim)
            column = pl.ds(pl.multiple_of(head * head_dim, head_dim), head_dim)
            lines = [head * tiles_here + tile for tile in range(tiles_here)]
            limits = [halo_ref[line, HALO_SLOTS - 1] for line in lines]
            most = most_of(limits)

            def work(cap):
                begun = []
                for tile in range(tiles_here):
                    here = slice(tile * tile_len, (tile + 1) * tile_len)
                    used = min(cap, needs[tile] + needs[tile] % 2)
                    if not used:
                        out_ref[here, column] = mixed_ref[here, column].astype(jnp.bfloat16)
                        continue
                    places = [halo_ref[lines[tile], slot] for slot in range(used)]
                    scores, largest = scores_of(
                        query_rows[here, :],
                        [tile_rows(key_rows, at, halo_tiles, tile_len) for at in places],
                        limits[tile],
                        0,
                    )
                    level = stats_ref[here, column]
                    newest = jnp.maximum(level, jnp.max(largest, axis=1, keepdims=True) * factor)
                    begun.append((here, places, scores, newest, jnp.exp2(level - newest)))
                for here, places, scores, newest, fade in begun:
                    added, update = mix(
                        scores,
                        newest,
                        factor,
                        [tile_rows(value_rows, at, halo_tiles, tile_len) for at in places],
                    )
                    out_ref[here, column] = (
                        (mixed_ref[here, column] * fade + update) / (fade + added)
                    ).astype(jnp.bfloat16)

            for cap in range(0, HALO_SLOTS - 1, 2):
                @pl.when((most + 1) // 2 == cap // 2)
                def _():
                    work(cap)

    smem = pl.BlockSpec(memory_space=pltpu.SMEM)
    hbm = pl.BlockSpec(memory_space=pl.ANY)
    vmem = pl.BlockSpec(memory_space=pltpu.VMEM)
    pairs = heads * tiles_here * (HALO_SLOTS - 2) // 2
    return pl.pallas_call(
        kernel,
        in_specs=[smem, smem] + [hbm] * 6 + [vmem, vmem],
        out_specs=vmem,
        out_shape=jax.ShapeDtypeStruct((rows, heads * head_dim), jnp.bfloat16),
        scratch_shapes=[
            pltpu.VMEM((2, heads, 2 * half, tokens, head_dim), jnp.bfloat16),
            pltpu.VMEM((heads, sources, tokens, head_dim), jnp.bfloat16),
            pltpu.SemaphoreType.DMA((heads, 5)),
        ],
        compiler_params=pltpu.CompilerParams(vmem_limit_bytes=VMEM_BYTES // 3),
        cost_estimate=pl.CostEstimate(
            flops=4 * pairs * tile_len * tile_len * head_dim,
            bytes_accessed=2 * heads * head_dim * (2 * halo_rows + 6 * rows),
            transcendentals=pairs * tile_len * tile_len,
        ),
    )(halo, kinds, query, *outer, *crossed, inner, mixed, stats)


def routes(blocks, group_size):
    def on(block):
        there = block + 1
        if there % ROW == 0:
            there = block + 1 - ROW if odd_row(block) == 0 else block + 1 + ROW
        return there

    def back(block):
        there = block - 1
        if block % ROW == 0:
            there = block - 1 + ROW if odd_row(block) == 1 else block - 1 - ROW
        return there

    outer, inner, across = [], [], []
    for block in range(blocks):
        odd_place = block % 2 == 1
        for pairs, there in (
            (outer, on(block) if odd_place else back(block)),
            (inner, back(block) if odd_place else on(block)),
        ):
            if 0 <= there < blocks:
                pairs += [(block * group_size + m, there * group_size + m) for m in range(group_size)]
        if block % ROW in (0, ROW - 1):
            other = block + ROW if odd_row(block) == 0 else block - ROW
            across += [
                tuple(at * group_size + owner_of(at, head_block, group_size) for at in (block, other))
                for head_block in range(group_size)
            ]
    return outer, inner, across


def assemble(parts):
    members, tokens, width = parts.shape
    step = tokens // 2

    def kernel(parts_ref, out_ref):
        odd = odd_row(lax.axis_index("seq"))
        for member in range(members):
            column = pl.multiple_of(owner_block(member, odd, members) * width, width)
            out_ref[:, pl.ds(column, width)] = parts_ref[member]

    return pl.pallas_call(
        kernel,
        grid=(tokens // step,),
        in_specs=[pl.BlockSpec((members, step, width), lambda g: (0, g, 0))],
        out_specs=pl.BlockSpec((step, members * width), lambda g: (g, 0)),
        out_shape=jax.ShapeDtypeStruct((tokens, members * width), parts.dtype),
        compiler_params=pltpu.CompilerParams(vmem_limit_bytes=VMEM_BYTES),
        cost_estimate=pl.CostEstimate(
            flops=0, bytes_accessed=4 * tokens * members * width, transcendentals=0
        ),
    )(parts)


def body(queries, keys, values, neighbours, counts):
    group_size = lax.axis_size("head")
    blocks = lax.axis_size("seq")
    local_tokens, feature_width = queries.shape
    head_count, tiles_here = counts.shape
    head_dim = feature_width // head_count
    per_device = head_count // group_size
    tile_len = local_tokens * group_size // tiles_here
    half = group_size // 2
    halo_tiles = half * local_tokens // tile_len

    def exchange(array):
        return lax.all_to_all(array, "head", split_axis=0, concat_axis=0, tiled=True)

    own = exchange(prepare([keys, values], [True, False], group_size, per_device, head_dim))
    block = lax.axis_index("seq")
    head_block = owner_block(lax.axis_index("head"), odd_row(block), group_size)
    place = jnp.stack([head_block * per_device, block * tiles_here]).astype(jnp.int32)
    x = block % ROW
    odd_place = x % 2 == 1
    kinds = jnp.stack(
        [
            jnp.where(odd_place, INNER, jnp.where(x == 0, CROSSED, OUTER)),
            jnp.where(odd_place, jnp.where(x == ROW - 1, CROSSED, OUTER), INNER),
        ]
    ).astype(jnp.int32)
    listed = neighbours.reshape(head_count, -1)
    inside, halo = sort_lists(listed, counts, place, tiles_here, per_device, halo_tiles)
    queries, inside, halo, kinds = lax.optimization_barrier((queries, inside, halo, kinds))
    query = exchange(prepare([queries], [True], group_size, per_device, head_dim))
    outer_route, inner_route, across = routes(blocks, group_size)
    both = ("seq", "head")
    first = jnp.where(odd_place, half, 0)
    outer_part = lax.dynamic_slice_in_dim(own, first, half, 0)
    inner_part = lax.dynamic_slice_in_dim(own, half - first, half, 0)
    outer = [lax.ppermute(outer_part[:, index], both, outer_route) for index in range(2)]
    inner = lax.ppermute(inner_part, both, inner_route)
    crossed = [lax.ppermute(part, both, across) for part in outer]
    mixed, stats = attend_local(own, query, inside, tile_len)
    result = attend_halo(query, outer, inner, crossed, mixed, stats, halo, kinds, tile_len)
    result = exchange(result.reshape(group_size, local_tokens, per_device * head_dim))
    return assemble(result)


def solution(mesh):
    placed = (
        P(("seq", "head"), None),
        P(("seq", "head"), None),
        P(("seq", "head"), None),
        P(None, "seq", None),
        P(None, "seq"),
    )
    return jax.shard_map(
        body, mesh=mesh, in_specs=placed, out_specs=P(("seq", "head"), None), check_vma=False
    )
```

```python
import math

import jax
import jax.numpy as jnp
from jax import lax
from jax.experimental import pallas as pl
from jax.experimental.pallas import tpu as pltpu
from jax.sharding import PartitionSpec as P

VMEM_BYTES = 60 * 1024 * 1024
ROW = 4
STEP_TILES = 6
OWN_SLOTS = 16
INNER, OUTER, CROSSED = range(3)
HALO_SLOTS = 8


def sign_block(size):
    row = lax.broadcasted_iota(jnp.int32, (size, size), 0)
    column = lax.broadcasted_iota(jnp.int32, (size, size), 1)
    common = jnp.bitwise_and(row, column)
    parity = jnp.zeros((size, size), jnp.int32)
    for bit_level in range(max(size.bit_length() - 1, 1)):
        parity = parity + jnp.bitwise_and(jnp.right_shift(common, bit_level), 1)
    return (1 - 2 * jnp.bitwise_and(parity, 1)).astype(jnp.float32).astype(jnp.bfloat16)


def odd_row(block):
    return (block // ROW) % 2


def owner_block(member, odd, group_size):
    return ((member // 2 + (member % 2) * odd) % (group_size // 2)) * 2 + member % 2


def owner_of(block, head_block, group_size):
    shift = (head_block % 2) * odd_row(block)
    return ((head_block // 2 - shift) % (group_size // 2)) * 2 + head_block % 2


def prepare(arrays, rotated, group_size, per_device, head_dim):
    tokens, width = arrays[0].shape
    count = len(arrays)
    step = tokens // 2
    scale = 1.0 / math.sqrt(head_dim)

    def kernel(*refs):
        out_ref, sign_ref = refs[-2:]

        @pl.when(pl.program_id(0) == 0)
        def _():
            sign_ref[...] = sign_block(head_dim)

        odd = odd_row(lax.axis_index("seq"))
        for index, ref in enumerate(refs[:-2]):
            for group in range(group_size):
                first = owner_block(group, odd, group_size) * per_device
                for head in range(per_device):
                    column = pl.multiple_of((first + head) * head_dim, head_dim)
                    block = ref[:, pl.ds(column, head_dim)]
                    if rotated[index]:
                        turned = jnp.dot(block, sign_ref[...], preferred_element_type=jnp.float32)
                        block = (turned * scale).astype(jnp.bfloat16)
                    out_ref[group, index, head] = block

    return pl.pallas_call(
        kernel,
        grid=(tokens // step,),
        in_specs=[pl.BlockSpec((step, width), lambda g: (g, 0))] * count,
        out_specs=pl.BlockSpec(
            (group_size, count, per_device, step, head_dim), lambda g: (0, 0, 0, g, 0)
        ),
        out_shape=jax.ShapeDtypeStruct(
            (group_size, count, per_device, tokens, head_dim), jnp.bfloat16
        ),
        scratch_shapes=[pltpu.VMEM((head_dim, head_dim), jnp.bfloat16)],
        compiler_params=pltpu.CompilerParams(vmem_limit_bytes=VMEM_BYTES),
        cost_estimate=pl.CostEstimate(
            flops=2 * tokens * width * head_dim * sum(rotated),
            bytes_accessed=4 * tokens * width * count,
            transcendentals=0,
        ),
    )(*arrays)


def scores_of(query_now, keys_of, limit, first_active):
    scores = []
    largest = None
    for slot in range(0, len(keys_of), 2):
        keys_now = jnp.concatenate([keys_of[slot](), keys_of[slot + 1]()], axis=0)
        pair = lax.dot_general(
            query_now, keys_now, (((1,), (1,)), ((), ())), preferred_element_type=jnp.float32
        )
        half = pair.shape[1] // 2
        one, two = pair[:, :half], pair[:, half:]
        if slot >= first_active:
            one = jnp.where(limit > slot, one, -jnp.inf)
        two = jnp.where(limit > slot + 1, two, -jnp.inf)
        scores += [one, two]
        larger = jnp.maximum(one, two)
        largest = larger if largest is None else jnp.maximum(largest, larger)
    return scores, largest


def mix(scores, level, factor, values_of):
    total = None
    mixed = None
    for slot in range(0, len(scores), 2):
        one = jnp.exp2(scores[slot] * factor - level)
        two = jnp.exp2(scores[slot + 1] * factor - level)
        both = one + two
        total = both if total is None else total + both
        weights = jnp.concatenate([one.astype(jnp.bfloat16), two.astype(jnp.bfloat16)], axis=1)
        values_now = jnp.concatenate([values_of[slot](), values_of[slot + 1]()], axis=0)
        update = jnp.dot(weights, values_now, preferred_element_type=jnp.float32)
        mixed = update if mixed is None else mixed + update
    return jnp.sum(total, axis=1, keepdims=True), mixed


def tile_rows(ref, at, count, tile_len):
    at = jnp.clip(at, 0, count - 1)
    return lambda: ref[pl.ds(pl.multiple_of(at * tile_len, tile_len), tile_len), :]


def sort_lists(listed, counts, place, tiles_here, heads, reach):
    slots = listed.shape[1] // tiles_here

    def kernel(place_ref, listed_ref, counts_ref, inside_ref, halo_ref):
        first_head = place_ref[0]
        first_tile = place_ref[1]

        @pl.loop(0, heads)
        def _(head):
            @pl.loop(0, tiles_here)
            def _(tile):
                line = head * tiles_here + tile
                limit = counts_ref[first_head + head, tile]
                for spare in range(OWN_SLOTS):
                    inside_ref[line, spare] = 0
                for spare in range(HALO_SLOTS):
                    halo_ref[line, spare] = 0
                inside = jnp.int32(0)
                outside = jnp.int32(0)
                for slot in range(slots):
                    at = listed_ref[first_head + head, tile * slots + slot] - first_tile
                    is_inside = (at >= 0) & (at < tiles_here)
                    active = slot < limit

                    @pl.when(active & is_inside)
                    def _():
                        inside_ref[line, inside] = at

                    @pl.when(active & ~is_inside)
                    def _():
                        halo_ref[line, jnp.minimum(outside, HALO_SLOTS - 2)] = jnp.where(
                            at < 0, at + reach, at - tiles_here + reach
                        )

                    inside = inside + (active & is_inside).astype(jnp.int32)
                    outside = outside + (active & ~is_inside).astype(jnp.int32)
                inside_ref[line, OWN_SLOTS - 1] = inside
                halo_ref[line, HALO_SLOTS - 1] = outside

    smem = pl.BlockSpec(memory_space=pltpu.SMEM)
    lines = heads * tiles_here
    return pl.pallas_call(
        kernel,
        in_specs=[smem, smem, smem],
        out_specs=[smem, smem],
        out_shape=[
            jax.ShapeDtypeStruct((lines, OWN_SLOTS), jnp.int32),
            jax.ShapeDtypeStruct((lines, HALO_SLOTS), jnp.int32),
        ],
    )(place, listed, counts)


def tiles_of_step(step, tiles_here):
    first = [STEP_TILES // 2 * step + number for number in range(STEP_TILES // 2)]
    return first + [tiles_here - 1 - tile for tile in first]


def most_of(limits):
    most = limits[0]
    for limit in limits[1:]:
        most = jnp.maximum(most, limit)
    return most


def attend_local(own, query, inside, tile_len):
    sources, _, heads, tokens, head_dim = own.shape
    rows = sources * tokens
    tiles_here = rows // tile_len
    slots = tiles_here
    factor = math.log2(math.e) / math.sqrt(head_dim)

    def kernel(inside_ref, own_ref, query_ref, mixed_ref, stats_ref, buf, sems):
        def copies(head):
            pairs = [(own_ref, 0), (own_ref, 1), (query_ref, 0)]
            return [
                pltpu.make_async_copy(
                    ref.at[:, index, head], buf.at[number, head], sems.at[head, number]
                )
                for number, (ref, index) in enumerate(pairs)
            ]

        for head in range(heads):
            for copy in copies(head):
                copy.start()

        @pl.loop(0, heads)
        def _(head):
            for copy in copies(head):
                copy.wait()
            key_rows, value_rows, query_rows = [
                buf.at[number, head].reshape(rows, head_dim) for number in range(3)
            ]
            column = pl.ds(pl.multiple_of(head * head_dim, head_dim), head_dim)

            @pl.loop(0, tiles_here // STEP_TILES)
            def _(step):
                tiles = tiles_of_step(step, tiles_here)
                lines = [head * tiles_here + tile for tile in tiles]
                limits = [inside_ref[line, OWN_SLOTS - 1] for line in lines]
                most = most_of(limits)

                def work(used):
                    begun = []
                    for line, tile, limit in zip(lines, tiles, limits):
                        here = pl.ds(pl.multiple_of(tile * tile_len, tile_len), tile_len)
                        places = [inside_ref[line, slot] for slot in range(used)]
                        scores, largest = scores_of(
                            query_rows[here, :],
                            [tile_rows(key_rows, at, tiles_here, tile_len) for at in places],
                            limit,
                            1,
                        )
                        peak = jnp.max(largest, axis=1, keepdims=True) * factor
                        begun.append((here, places, scores, peak))
                    for here, places, scores, peak in begun:
                        total, mixed = mix(
                            scores,
                            peak,
                            factor,
                            [tile_rows(value_rows, at, tiles_here, tile_len) for at in places],
                        )
                        mixed_ref[here, column] = mixed / total
                        stats_ref[here, column] = jnp.broadcast_to(
                            peak + jnp.log2(total), (tile_len, head_dim)
                        )

                for used in range(2, slots + 1, 2):
                    @pl.when((most + 1) // 2 == used // 2)
                    def _():
                        work(used)

    smem = pl.BlockSpec(memory_space=pltpu.SMEM)
    hbm = pl.BlockSpec(memory_space=pl.ANY)
    vmem = pl.BlockSpec(memory_space=pltpu.VMEM)
    pairs = heads * tiles_here * slots
    state = jax.ShapeDtypeStruct((rows, heads * head_dim), jnp.float32)
    return pl.pallas_call(
        kernel,
        in_specs=[smem, hbm, hbm],
        out_specs=[vmem, vmem],
        out_shape=[state, state],
        scratch_shapes=[
            pltpu.VMEM((3, heads, sources, tokens, head_dim), jnp.bfloat16),
            pltpu.SemaphoreType.DMA((heads, 3)),
        ],
        compiler_params=pltpu.CompilerParams(vmem_limit_bytes=VMEM_BYTES // 3),
        cost_estimate=pl.CostEstimate(
            flops=4 * pairs * tile_len * tile_len * head_dim,
            bytes_accessed=2 * heads * head_dim * 7 * rows,
            transcendentals=pairs * tile_len * tile_len,
        ),
    )(inside, own, query)


def attend_halo(query, outer, inner, crossed, mixed, stats, halo, kinds, tile_len):
    sources, _, heads, tokens, head_dim = query.shape
    half = inner.shape[0]
    rows = sources * tokens
    halo_rows = 2 * half * tokens
    halo_tiles = halo_rows // tile_len
    reach = halo_tiles // 2
    tiles_here = rows // tile_len
    factor = math.log2(math.e) / math.sqrt(head_dim)
    needs = [max(reach - tile, tile - tiles_here + 1 + reach) for tile in range(tiles_here)]

    def kernel(halo_ref, kinds_ref, query_ref, outer_k, outer_v, crossed_k, crossed_v, inner_ref,
               mixed_ref, stats_ref, out_ref, buf, query_buf, sems):
        def query_copy(head):
            return pltpu.make_async_copy(
                query_ref.at[:, 0, head], query_buf.at[head], sems.at[head, 0]
            )

        def side_copy(head, index, side, kind):
            if kind == INNER:
                source = inner_ref.at[:, index, head]
            elif kind == OUTER:
                source = (outer_k, outer_v)[index].at[:, head]
            else:
                source = (crossed_k, crossed_v)[index].at[:, head]
            return pltpu.make_async_copy(
                source,
                buf.at[index, head, pl.ds(side * half, half)],
                sems.at[head, 1 + 2 * index + side],
            )

        for head in range(heads):
            query_copy(head).start()
            for side in range(2):
                for kind in (INNER, OUTER, CROSSED):
                    @pl.when(kinds_ref[side] == kind)
                    def _():
                        for index in range(2):
                            side_copy(head, index, side, kind).start()

        @pl.loop(0, heads)
        def _(head):
            query_copy(head).wait()
            for side in range(2):
                side_copy(head, 0, side, INNER).wait()
            key_rows, value_rows = [
                buf.at[index, head].reshape(halo_rows, head_dim) for index in range(2)
            ]
            query_rows = query_buf.at[head].reshape(rows, head_dim)
            column = pl.ds(pl.multiple_of(head * head_dim, head_dim), head_dim)
            lines = [head * tiles_here + tile for tile in range(tiles_here)]
            limits = [halo_ref[line, HALO_SLOTS - 1] for line in lines]
            most = most_of(limits)

            def work(cap):
                begun = []
                for tile in range(tiles_here):
                    here = slice(tile * tile_len, (tile + 1) * tile_len)
                    used = min(cap, needs[tile] + needs[tile] % 2)
                    if not used:
                        out_ref[here, column] = mixed_ref[here, column].astype(jnp.bfloat16)
                        continue
                    places = [halo_ref[lines[tile], slot] for slot in range(used)]
                    scores, largest = scores_of(
                        query_rows[here, :],
                        [tile_rows(key_rows, at, halo_tiles, tile_len) for at in places],
                        limits[tile],
                        0,
                    )
                    level = stats_ref[here, column]
                    newest = jnp.maximum(level, jnp.max(largest, axis=1, keepdims=True) * factor)
                    begun.append((here, places, scores, newest, jnp.exp2(level - newest)))
                for side in range(2):
                    side_copy(head, 1, side, INNER).wait()
                for here, places, scores, newest, fade in begun:
                    added, update = mix(
                        scores,
                        newest,
                        factor,
                        [tile_rows(value_rows, at, halo_tiles, tile_len) for at in places],
                    )
                    out_ref[here, column] = (
                        (mixed_ref[here, column] * fade + update) / (fade + added)
                    ).astype(jnp.bfloat16)

            for cap in range(0, HALO_SLOTS - 1, 2):
                @pl.when((most + 1) // 2 == cap // 2)
                def _():
                    work(cap)

    smem = pl.BlockSpec(memory_space=pltpu.SMEM)
    hbm = pl.BlockSpec(memory_space=pl.ANY)
    vmem = pl.BlockSpec(memory_space=pltpu.VMEM)
    pairs = heads * tiles_here * (HALO_SLOTS - 2) // 2
    return pl.pallas_call(
        kernel,
        in_specs=[smem, smem] + [hbm] * 6 + [vmem, vmem],
        out_specs=vmem,
        out_shape=jax.ShapeDtypeStruct((rows, heads * head_dim), jnp.bfloat16),
        scratch_shapes=[
            pltpu.VMEM((2, heads, 2 * half, tokens, head_dim), jnp.bfloat16),
            pltpu.VMEM((heads, sources, tokens, head_dim), jnp.bfloat16),
            pltpu.SemaphoreType.DMA((heads, 5)),
        ],
        compiler_params=pltpu.CompilerParams(vmem_limit_bytes=VMEM_BYTES // 3),
        cost_estimate=pl.CostEstimate(
            flops=4 * pairs * tile_len * tile_len * head_dim,
            bytes_accessed=2 * heads * head_dim * (2 * halo_rows + 6 * rows),
            transcendentals=pairs * tile_len * tile_len,
        ),
    )(halo, kinds, query, *outer, *crossed, inner, mixed, stats)


def routes(blocks, group_size):
    def on(block):
        there = block + 1
        if there % ROW == 0:
            there = block + 1 - ROW if odd_row(block) == 0 else block + 1 + ROW
        return there

    def back(block):
        there = block - 1
        if block % ROW == 0:
            there = block - 1 + ROW if odd_row(block) == 1 else block - 1 - ROW
        return there

    outer, inner, across = [], [], []
    for block in range(blocks):
        odd_place = block % 2 == 1
        for pairs, there in (
            (outer, on(block) if odd_place else back(block)),
            (inner, back(block) if odd_place else on(block)),
        ):
            if 0 <= there < blocks:
                pairs += [(block * group_size + m, there * group_size + m) for m in range(group_size)]
        if block % ROW in (0, ROW - 1):
            other = block + ROW if odd_row(block) == 0 else block - ROW
            across += [
                tuple(at * group_size + owner_of(at, head_block, group_size) for at in (block, other))
                for head_block in range(group_size)
            ]
    return outer, inner, across


def assemble(parts):
    members, tokens, width = parts.shape
    step = tokens // 2

    def kernel(parts_ref, out_ref):
        odd = odd_row(lax.axis_index("seq"))
        for member in range(members):
            column = pl.multiple_of(owner_block(member, odd, members) * width, width)
            out_ref[:, pl.ds(column, width)] = parts_ref[member]

    return pl.pallas_call(
        kernel,
        grid=(tokens // step,),
        in_specs=[pl.BlockSpec((members, step, width), lambda g: (0, g, 0))],
        out_specs=pl.BlockSpec((step, members * width), lambda g: (g, 0)),
        out_shape=jax.ShapeDtypeStruct((tokens, members * width), parts.dtype),
        compiler_params=pltpu.CompilerParams(vmem_limit_bytes=VMEM_BYTES),
        cost_estimate=pl.CostEstimate(
            flops=0, bytes_accessed=4 * tokens * members * width, transcendentals=0
        ),
    )(parts)


def body(queries, keys, values, neighbours, counts):
    group_size = lax.axis_size("head")
    blocks = lax.axis_size("seq")
    local_tokens, feature_width = queries.shape
    head_count, tiles_here = counts.shape
    head_dim = feature_width // head_count
    per_device = head_count // group_size
    tile_len = local_tokens * group_size // tiles_here
    half = group_size // 2
    halo_tiles = half * local_tokens // tile_len

    def exchange(array):
        return lax.all_to_all(array, "head", split_axis=0, concat_axis=0, tiled=True)

    own = exchange(prepare([keys, values], [True, False], group_size, per_device, head_dim))
    block = lax.axis_index("seq")
    head_block = owner_block(lax.axis_index("head"), odd_row(block), group_size)
    place = jnp.stack([head_block * per_device, block * tiles_here]).astype(jnp.int32)
    x = block % ROW
    odd_place = x % 2 == 1
    kinds = jnp.stack(
        [
            jnp.where(odd_place, INNER, jnp.where(x == 0, CROSSED, OUTER)),
            jnp.where(odd_place, jnp.where(x == ROW - 1, CROSSED, OUTER), INNER),
        ]
    ).astype(jnp.int32)
    listed = neighbours.reshape(head_count, -1)
    inside, halo = sort_lists(listed, counts, place, tiles_here, per_device, halo_tiles)
    queries, inside, halo, kinds = lax.optimization_barrier((queries, inside, halo, kinds))
    query = exchange(prepare([queries], [True], group_size, per_device, head_dim))
    outer_route, inner_route, across = routes(blocks, group_size)
    both = ("seq", "head")
    first = jnp.where(odd_place, half, 0)
    outer_part = lax.dynamic_slice_in_dim(own, first, half, 0)
    inner_part = lax.dynamic_slice_in_dim(own, half - first, half, 0)
    outer = [lax.ppermute(outer_part[:, index], both, outer_route) for index in range(2)]
    inner = lax.ppermute(inner_part, both, inner_route)
    crossed = [lax.ppermute(part, both, across) for part in outer]
    mixed, stats = attend_local(own, query, inside, tile_len)
    result = attend_halo(query, outer, inner, crossed, mixed, stats, halo, kinds, tile_len)
    result = exchange(result.reshape(group_size, local_tokens, per_device * head_dim))
    return assemble(result)


def solution(mesh):
    placed = (
        P(("seq", "head"), None),
        P(("seq", "head"), None),
        P(("seq", "head"), None),
        P(None, "seq", None),
        P(None, "seq"),
    )
    return jax.shard_map(
        body, mesh=mesh, in_specs=placed, out_specs=P(("seq", "head"), None), check_vma=False
    )
```

```python
import math

import jax
import jax.numpy as jnp
from jax import lax
from jax.experimental import pallas as pl
from jax.experimental.pallas import tpu as pltpu
from jax.sharding import PartitionSpec as P

VMEM_BYTES = 60 * 1024 * 1024
ROW = 4
STEP_TILES = 6
OWN_SLOTS = 16
INNER, OUTER, CROSSED = range(3)
HALO_SLOTS = 8


def sign_block(size):
    row = lax.broadcasted_iota(jnp.int32, (size, size), 0)
    column = lax.broadcasted_iota(jnp.int32, (size, size), 1)
    common = jnp.bitwise_and(row, column)
    parity = jnp.zeros((size, size), jnp.int32)
    for bit_level in range(max(size.bit_length() - 1, 1)):
        parity = parity + jnp.bitwise_and(jnp.right_shift(common, bit_level), 1)
    return (1 - 2 * jnp.bitwise_and(parity, 1)).astype(jnp.float32).astype(jnp.bfloat16)


def odd_row(block):
    return (block // ROW) % 2


def owner_block(member, odd, group_size):
    return ((member // 2 + (member % 2) * odd) % (group_size // 2)) * 2 + member % 2


def owner_of(block, head_block, group_size):
    shift = (head_block % 2) * odd_row(block)
    return ((head_block // 2 - shift) % (group_size // 2)) * 2 + head_block % 2


def prepare(arrays, rotated, group_size, per_device, head_dim):
    tokens, width = arrays[0].shape
    count = len(arrays)
    step = tokens // 2
    scale = 1.0 / math.sqrt(head_dim)

    def kernel(*refs):
        out_ref, sign_ref = refs[-2:]

        @pl.when(pl.program_id(0) == 0)
        def _():
            sign_ref[...] = sign_block(head_dim)

        odd = odd_row(lax.axis_index("seq"))
        for index, ref in enumerate(refs[:-2]):
            for group in range(group_size):
                first = owner_block(group, odd, group_size) * per_device
                for head in range(per_device):
                    column = pl.multiple_of((first + head) * head_dim, head_dim)
                    block = ref[:, pl.ds(column, head_dim)]
                    if rotated[index]:
                        turned = jnp.dot(block, sign_ref[...], preferred_element_type=jnp.float32)
                        block = (turned * scale).astype(jnp.bfloat16)
                    out_ref[group, index, head] = block

    return pl.pallas_call(
        kernel,
        grid=(tokens // step,),
        in_specs=[pl.BlockSpec((step, width), lambda g: (g, 0))] * count,
        out_specs=pl.BlockSpec(
            (group_size, count, per_device, step, head_dim), lambda g: (0, 0, 0, g, 0)
        ),
        out_shape=jax.ShapeDtypeStruct(
            (group_size, count, per_device, tokens, head_dim), jnp.bfloat16
        ),
        scratch_shapes=[pltpu.VMEM((head_dim, head_dim), jnp.bfloat16)],
        compiler_params=pltpu.CompilerParams(vmem_limit_bytes=VMEM_BYTES),
        cost_estimate=pl.CostEstimate(
            flops=2 * tokens * width * head_dim * sum(rotated),
            bytes_accessed=4 * tokens * width * count,
            transcendentals=0,
        ),
    )(*arrays)


def scores_of(query_now, keys_of, limit, first_active):
    scores = []
    largest = None
    for slot in range(0, len(keys_of), 2):
        keys_now = jnp.concatenate([keys_of[slot](), keys_of[slot + 1]()], axis=0)
        pair = lax.dot_general(
            query_now, keys_now, (((1,), (1,)), ((), ())), preferred_element_type=jnp.float32
        )
        half = pair.shape[1] // 2
        one, two = pair[:, :half], pair[:, half:]
        if slot >= first_active:
            one = jnp.where(limit > slot, one, -jnp.inf)
        two = jnp.where(limit > slot + 1, two, -jnp.inf)
        scores += [one, two]
        larger = jnp.maximum(one, two)
        largest = larger if largest is None else jnp.maximum(largest, larger)
    return scores, largest


def mix(scores, level, factor, values_of):
    total = None
    mixed = None
    for slot in range(0, len(scores), 2):
        one = jnp.exp2(scores[slot] * factor - level)
        two = jnp.exp2(scores[slot + 1] * factor - level)
        both = one + two
        total = both if total is None else total + both
        weights = jnp.concatenate([one.astype(jnp.bfloat16), two.astype(jnp.bfloat16)], axis=1)
        values_now = jnp.concatenate([values_of[slot](), values_of[slot + 1]()], axis=0)
        update = jnp.dot(weights, values_now, preferred_element_type=jnp.float32)
        mixed = update if mixed is None else mixed + update
    return jnp.sum(total, axis=1, keepdims=True), mixed


def tile_rows(ref, at, count, tile_len):
    at = jnp.clip(at, 0, count - 1)
    return lambda: ref[pl.ds(pl.multiple_of(at * tile_len, tile_len), tile_len), :]


def sort_lists(listed, counts, place, tiles_here, heads, reach):
    slots = listed.shape[1] // tiles_here

    def kernel(place_ref, listed_ref, counts_ref, inside_ref, halo_ref):
        first_head = place_ref[0]
        first_tile = place_ref[1]

        @pl.loop(0, heads)
        def _(head):
            @pl.loop(0, tiles_here)
            def _(tile):
                line = head * tiles_here + tile
                limit = counts_ref[first_head + head, tile]
                for spare in range(OWN_SLOTS):
                    inside_ref[line, spare] = 0
                for spare in range(HALO_SLOTS):
                    halo_ref[line, spare] = 0
                inside = jnp.int32(0)
                outside = jnp.int32(0)
                for slot in range(slots):
                    at = listed_ref[first_head + head, tile * slots + slot] - first_tile
                    is_inside = (at >= 0) & (at < tiles_here)
                    active = slot < limit

                    @pl.when(active & is_inside)
                    def _():
                        inside_ref[line, inside] = at

                    @pl.when(active & ~is_inside)
                    def _():
                        halo_ref[line, jnp.minimum(outside, HALO_SLOTS - 2)] = jnp.where(
                            at < 0, at + reach, at - tiles_here + reach
                        )

                    inside = inside + (active & is_inside).astype(jnp.int32)
                    outside = outside + (active & ~is_inside).astype(jnp.int32)
                inside_ref[line, OWN_SLOTS - 1] = inside
                halo_ref[line, HALO_SLOTS - 1] = outside

    smem = pl.BlockSpec(memory_space=pltpu.SMEM)
    lines = heads * tiles_here
    return pl.pallas_call(
        kernel,
        in_specs=[smem, smem, smem],
        out_specs=[smem, smem],
        out_shape=[
            jax.ShapeDtypeStruct((lines, OWN_SLOTS), jnp.int32),
            jax.ShapeDtypeStruct((lines, HALO_SLOTS), jnp.int32),
        ],
    )(place, listed, counts)


def tiles_of_step(step, tiles_here):
    first = [STEP_TILES // 2 * step + number for number in range(STEP_TILES // 2)]
    return first + [tiles_here - 1 - tile for tile in first]


def most_of(limits):
    most = limits[0]
    for limit in limits[1:]:
        most = jnp.maximum(most, limit)
    return most


def attend_local(own, query, inside, tile_len):
    sources, _, heads, tokens, head_dim = own.shape
    rows = sources * tokens
    tiles_here = rows // tile_len
    slots = tiles_here
    factor = math.log2(math.e) / math.sqrt(head_dim)

    def kernel(inside_ref, own_ref, query_ref, mixed_ref, stats_ref, buf, sems):
        def copies(head):
            pairs = [(own_ref, 0), (own_ref, 1), (query_ref, 0)]
            return [
                pltpu.make_async_copy(
                    ref.at[:, index, head], buf.at[number, head], sems.at[head, number]
                )
                for number, (ref, index) in enumerate(pairs)
            ]

        for head in range(heads):
            for copy in copies(head):
                copy.start()

        @pl.loop(0, heads)
        def _(head):
            for copy in copies(head):
                copy.wait()
            key_rows, value_rows, query_rows = [
                buf.at[number, head].reshape(rows, head_dim) for number in range(3)
            ]
            column = pl.ds(pl.multiple_of(head * head_dim, head_dim), head_dim)

            @pl.loop(0, tiles_here // STEP_TILES)
            def _(step):
                tiles = tiles_of_step(step, tiles_here)
                lines = [head * tiles_here + tile for tile in tiles]
                limits = [inside_ref[line, OWN_SLOTS - 1] for line in lines]
                most = most_of(limits)

                def work(used):
                    begun = []
                    for line, tile, limit in zip(lines, tiles, limits):
                        here = pl.ds(pl.multiple_of(tile * tile_len, tile_len), tile_len)
                        places = [inside_ref[line, slot] for slot in range(used)]
                        scores, largest = scores_of(
                            query_rows[here, :],
                            [tile_rows(key_rows, at, tiles_here, tile_len) for at in places],
                            limit,
                            1,
                        )
                        peak = jnp.max(largest, axis=1, keepdims=True) * factor
                        begun.append((here, places, scores, peak))
                    for here, places, scores, peak in begun:
                        total, mixed = mix(
                            scores,
                            peak,
                            factor,
                            [tile_rows(value_rows, at, tiles_here, tile_len) for at in places],
                        )
                        mixed_ref[here, column] = mixed / total
                        stats_ref[here, column] = jnp.broadcast_to(
                            peak + jnp.log2(total), (tile_len, head_dim)
                        )

                for used in range(2, slots + 1, 2):
                    @pl.when((most + 1) // 2 == used // 2)
                    def _():
                        work(used)

    smem = pl.BlockSpec(memory_space=pltpu.SMEM)
    hbm = pl.BlockSpec(memory_space=pl.ANY)
    vmem = pl.BlockSpec(memory_space=pltpu.VMEM)
    pairs = heads * tiles_here * slots
    state = jax.ShapeDtypeStruct((rows, heads * head_dim), jnp.float32)
    return pl.pallas_call(
        kernel,
        in_specs=[smem, hbm, hbm],
        out_specs=[vmem, vmem],
        out_shape=[state, state],
        scratch_shapes=[
            pltpu.VMEM((3, heads, sources, tokens, head_dim), jnp.bfloat16),
            pltpu.SemaphoreType.DMA((heads, 3)),
        ],
        compiler_params=pltpu.CompilerParams(vmem_limit_bytes=VMEM_BYTES // 3),
        cost_estimate=pl.CostEstimate(
            flops=4 * pairs * tile_len * tile_len * head_dim,
            bytes_accessed=2 * heads * head_dim * 7 * rows,
            transcendentals=pairs * tile_len * tile_len,
        ),
    )(inside, own, query)


def attend_halo(query, outer, inner, crossed, mixed, stats, halo, kinds, tile_len):
    sources, _, heads, tokens, head_dim = query.shape
    half = inner.shape[0]
    rows = sources * tokens
    halo_rows = 2 * half * tokens
    halo_tiles = halo_rows // tile_len
    reach = halo_tiles // 2
    tiles_here = rows // tile_len
    factor = math.log2(math.e) / math.sqrt(head_dim)
    needs = [max(reach - tile, tile - tiles_here + 1 + reach) for tile in range(tiles_here)]

    def kernel(halo_ref, kinds_ref, query_ref, outer_k, outer_v, crossed_k, crossed_v, inner_ref,
               mixed_ref, stats_ref, out_ref, buf, query_buf, sems):
        def query_copy(head):
            return pltpu.make_async_copy(
                query_ref.at[:, 0, head], query_buf.at[head], sems.at[head, 0]
            )

        def side_copy(head, index, side, kind):
            if kind == INNER:
                source = inner_ref.at[:, index, head]
            elif kind == OUTER:
                source = (outer_k, outer_v)[index].at[:, head]
            else:
                source = (crossed_k, crossed_v)[index].at[:, head]
            return pltpu.make_async_copy(
                source,
                buf.at[index, head, pl.ds(side * half, half)],
                sems.at[head, 1 + 2 * index + side],
            )

        for head in range(heads):
            query_copy(head).start()
            for side in range(2):
                for kind in (INNER, OUTER, CROSSED):
                    @pl.when(kinds_ref[side] == kind)
                    def _():
                        for index in range(2):
                            side_copy(head, index, side, kind).start()

        @pl.loop(0, heads)
        def _(head):
            query_copy(head).wait()
            for side in range(2):
                side_copy(head, 0, side, INNER).wait()
            key_rows, value_rows = [
                buf.at[index, head].reshape(halo_rows, head_dim) for index in range(2)
            ]
            query_rows = query_buf.at[head].reshape(rows, head_dim)
            column = pl.ds(pl.multiple_of(head * head_dim, head_dim), head_dim)
            lines = [head * tiles_here + tile for tile in range(tiles_here)]
            limits = [halo_ref[line, HALO_SLOTS - 1] for line in lines]
            most = most_of(limits)

            def work(cap):
                begun = []
                for tile in range(tiles_here):
                    here = slice(tile * tile_len, (tile + 1) * tile_len)
                    used = min(cap, needs[tile] + needs[tile] % 2)
                    if not used:
                        out_ref[here, column] = mixed_ref[here, column].astype(jnp.bfloat16)
                        continue
                    places = [halo_ref[lines[tile], slot] for slot in range(used)]
                    scores, largest = scores_of(
                        query_rows[here, :],
                        [tile_rows(key_rows, at, halo_tiles, tile_len) for at in places],
                        limits[tile],
                        0,
                    )
                    level = stats_ref[here, column]
                    newest = jnp.maximum(level, jnp.max(largest, axis=1, keepdims=True) * factor)
                    begun.append((here, places, scores, newest, jnp.exp2(level - newest)))
                for side in range(2):
                    side_copy(head, 1, side, INNER).wait()
                for here, places, scores, newest, fade in begun:
                    added, update = mix(
                        scores,
                        newest,
                        factor,
                        [tile_rows(value_rows, at, halo_tiles, tile_len) for at in places],
                    )
                    out_ref[here, column] = (
                        (mixed_ref[here, column] * fade + update) / (fade + added)
                    ).astype(jnp.bfloat16)

            for cap in range(0, HALO_SLOTS - 1, 2):
                @pl.when((most + 1) // 2 == cap // 2)
                def _():
                    work(cap)

    smem = pl.BlockSpec(memory_space=pltpu.SMEM)
    hbm = pl.BlockSpec(memory_space=pl.ANY)
    vmem = pl.BlockSpec(memory_space=pltpu.VMEM)
    pairs = heads * tiles_here * (HALO_SLOTS - 2) // 2
    return pl.pallas_call(
        kernel,
        in_specs=[smem, smem] + [hbm] * 6 + [vmem, vmem],
        out_specs=vmem,
        out_shape=jax.ShapeDtypeStruct((rows, heads * head_dim), jnp.bfloat16),
        scratch_shapes=[
            pltpu.VMEM((2, heads, 2 * half, tokens, head_dim), jnp.bfloat16),
            pltpu.VMEM((heads, sources, tokens, head_dim), jnp.bfloat16),
            pltpu.SemaphoreType.DMA((heads, 5)),
        ],
        compiler_params=pltpu.CompilerParams(vmem_limit_bytes=VMEM_BYTES // 3),
        cost_estimate=pl.CostEstimate(
            flops=4 * pairs * tile_len * tile_len * head_dim,
            bytes_accessed=2 * heads * head_dim * (2 * halo_rows + 6 * rows),
            transcendentals=pairs * tile_len * tile_len,
        ),
    )(halo, kinds, query, *outer, *crossed, inner, mixed, stats)


def routes(blocks, group_size):
    def on(block):
        there = block + 1
        if there % ROW == 0:
            there = block + 1 - ROW if odd_row(block) == 0 else block + 1 + ROW
        return there

    def back(block):
        there = block - 1
        if block % ROW == 0:
            there = block - 1 + ROW if odd_row(block) == 1 else block - 1 - ROW
        return there

    outer, inner, across = [], [], []
    for block in range(blocks):
        odd_place = block % 2 == 1
        for pairs, there in (
            (outer, on(block) if odd_place else back(block)),
            (inner, back(block) if odd_place else on(block)),
        ):
            if 0 <= there < blocks:
                pairs += [(block * group_size + m, there * group_size + m) for m in range(group_size)]
        if block % ROW in (0, ROW - 1):
            other = block + ROW if odd_row(block) == 0 else block - ROW
            across += [
                tuple(at * group_size + owner_of(at, head_block, group_size) for at in (block, other))
                for head_block in range(group_size)
            ]
    return outer, inner, across


def assemble(parts):
    members, tokens, width = parts.shape
    step = tokens // 2

    def kernel(parts_ref, out_ref):
        odd = odd_row(lax.axis_index("seq"))
        first = pl.multiple_of(pl.program_id(0) * step, step)
        for member in range(members):
            column = pl.multiple_of(owner_block(member, odd, members) * width, width)
            out_ref[:, pl.ds(column, width)] = parts_ref[member, pl.ds(first, step), :]

    return pl.pallas_call(
        kernel,
        grid=(tokens // step,),
        in_specs=[pl.BlockSpec(memory_space=pltpu.VMEM)],
        out_specs=pl.BlockSpec((step, members * width), lambda g: (g, 0)),
        out_shape=jax.ShapeDtypeStruct((tokens, members * width), parts.dtype),
        compiler_params=pltpu.CompilerParams(vmem_limit_bytes=VMEM_BYTES // 3),
        cost_estimate=pl.CostEstimate(
            flops=0, bytes_accessed=4 * tokens * members * width, transcendentals=0
        ),
    )(parts)


def body(queries, keys, values, neighbours, counts):
    group_size = lax.axis_size("head")
    blocks = lax.axis_size("seq")
    local_tokens, feature_width = queries.shape
    head_count, tiles_here = counts.shape
    head_dim = feature_width // head_count
    per_device = head_count // group_size
    tile_len = local_tokens * group_size // tiles_here
    half = group_size // 2
    halo_tiles = half * local_tokens // tile_len

    def exchange(array):
        return lax.all_to_all(array, "head", split_axis=0, concat_axis=0, tiled=True)

    own = exchange(prepare([keys, values], [True, False], group_size, per_device, head_dim))
    block = lax.axis_index("seq")
    head_block = owner_block(lax.axis_index("head"), odd_row(block), group_size)
    place = jnp.stack([head_block * per_device, block * tiles_here]).astype(jnp.int32)
    x = block % ROW
    odd_place = x % 2 == 1
    kinds = jnp.stack(
        [
            jnp.where(odd_place, INNER, jnp.where(x == 0, CROSSED, OUTER)),
            jnp.where(odd_place, jnp.where(x == ROW - 1, CROSSED, OUTER), INNER),
        ]
    ).astype(jnp.int32)
    listed = neighbours.reshape(head_count, -1)
    inside, halo = sort_lists(listed, counts, place, tiles_here, per_device, halo_tiles)
    queries, inside, halo, kinds = lax.optimization_barrier((queries, inside, halo, kinds))
    query = exchange(prepare([queries], [True], group_size, per_device, head_dim))
    outer_route, inner_route, across = routes(blocks, group_size)
    both = ("seq", "head")
    first = jnp.where(odd_place, half, 0)
    outer_part = lax.dynamic_slice_in_dim(own, first, half, 0)
    inner_part = lax.dynamic_slice_in_dim(own, half - first, half, 0)
    outer = [lax.ppermute(outer_part[:, index], both, outer_route) for index in range(2)]
    inner = lax.ppermute(inner_part, both, inner_route)
    crossed = [lax.ppermute(part, both, across) for part in outer]
    mixed, stats = attend_local(own, query, inside, tile_len)
    result = attend_halo(query, outer, inner, crossed, mixed, stats, halo, kinds, tile_len)
    result = exchange(result.reshape(group_size, local_tokens, per_device * head_dim))
    return assemble(result)


def solution(mesh):
    placed = (
        P(("seq", "head"), None),
        P(("seq", "head"), None),
        P(("seq", "head"), None),
        P(None, "seq", None),
        P(None, "seq"),
    )
    return jax.shard_map(
        body, mesh=mesh, in_specs=placed, out_specs=P(("seq", "head"), None), check_vma=False
    )
```

```python
import math

import jax
import jax.numpy as jnp
from jax import lax
from jax.experimental import pallas as pl
from jax.experimental.pallas import tpu as pltpu
from jax.sharding import PartitionSpec as P

VMEM_BYTES = 60 * 1024 * 1024
ROW = 4
STEP_TILES = 6
OWN_SLOTS = 16
INNER, OUTER, CROSSED = range(3)
HALO_SLOTS = 8


def sign_block(size):
    row = lax.broadcasted_iota(jnp.int32, (size, size), 0)
    column = lax.broadcasted_iota(jnp.int32, (size, size), 1)
    common = jnp.bitwise_and(row, column)
    parity = jnp.zeros((size, size), jnp.int32)
    for bit_level in range(max(size.bit_length() - 1, 1)):
        parity = parity + jnp.bitwise_and(jnp.right_shift(common, bit_level), 1)
    return (1 - 2 * jnp.bitwise_and(parity, 1)).astype(jnp.float32).astype(jnp.bfloat16)


def odd_row(block):
    return (block // ROW) % 2


def owner_block(member, odd, group_size):
    return ((member // 2 + (member % 2) * odd) % (group_size // 2)) * 2 + member % 2


def owner_of(block, head_block, group_size):
    shift = (head_block % 2) * odd_row(block)
    return ((head_block // 2 - shift) % (group_size // 2)) * 2 + head_block % 2


def prepare(arrays, rotated, group_size, per_device, head_dim):
    tokens, width = arrays[0].shape
    count = len(arrays)
    step = tokens // 2
    scale = 1.0 / math.sqrt(head_dim)

    def kernel(*refs):
        out_ref, sign_ref = refs[-2:]

        @pl.when(pl.program_id(0) == 0)
        def _():
            sign_ref[...] = sign_block(head_dim)

        odd = odd_row(lax.axis_index("seq"))
        for index, ref in enumerate(refs[:-2]):
            for group in range(group_size):
                first = owner_block(group, odd, group_size) * per_device
                for head in range(per_device):
                    column = pl.multiple_of((first + head) * head_dim, head_dim)
                    block = ref[:, pl.ds(column, head_dim)]
                    if rotated[index]:
                        turned = jnp.dot(block, sign_ref[...], preferred_element_type=jnp.float32)
                        block = (turned * scale).astype(jnp.bfloat16)
                    out_ref[group, index, head] = block

    return pl.pallas_call(
        kernel,
        grid=(tokens // step,),
        in_specs=[pl.BlockSpec((step, width), lambda g: (g, 0))] * count,
        out_specs=pl.BlockSpec(
            (group_size, count, per_device, step, head_dim), lambda g: (0, 0, 0, g, 0)
        ),
        out_shape=jax.ShapeDtypeStruct(
            (group_size, count, per_device, tokens, head_dim), jnp.bfloat16
        ),
        scratch_shapes=[pltpu.VMEM((head_dim, head_dim), jnp.bfloat16)],
        compiler_params=pltpu.CompilerParams(vmem_limit_bytes=VMEM_BYTES),
        cost_estimate=pl.CostEstimate(
            flops=2 * tokens * width * head_dim * sum(rotated),
            bytes_accessed=4 * tokens * width * count,
            transcendentals=0,
        ),
    )(*arrays)


def scores_of(query_now, keys_of, limit, first_active):
    scores = []
    largest = None
    for slot in range(0, len(keys_of), 2):
        keys_now = jnp.concatenate([keys_of[slot](), keys_of[slot + 1]()], axis=0)
        pair = lax.dot_general(
            query_now, keys_now, (((1,), (1,)), ((), ())), preferred_element_type=jnp.float32
        )
        half = pair.shape[1] // 2
        one, two = pair[:, :half], pair[:, half:]
        if slot >= first_active:
            one = jnp.where(limit > slot, one, -jnp.inf)
        two = jnp.where(limit > slot + 1, two, -jnp.inf)
        scores += [one, two]
        larger = jnp.maximum(one, two)
        largest = larger if largest is None else jnp.maximum(largest, larger)
    return scores, largest


def mix(scores, level, factor, values_of):
    total = None
    mixed = None
    for slot in range(0, len(scores), 2):
        one = jnp.exp2(scores[slot] * factor - level)
        two = jnp.exp2(scores[slot + 1] * factor - level)
        both = one + two
        total = both if total is None else total + both
        weights = jnp.concatenate([one.astype(jnp.bfloat16), two.astype(jnp.bfloat16)], axis=1)
        values_now = jnp.concatenate([values_of[slot](), values_of[slot + 1]()], axis=0)
        update = jnp.dot(weights, values_now, preferred_element_type=jnp.float32)
        mixed = update if mixed is None else mixed + update
    return jnp.sum(total, axis=1, keepdims=True), mixed


def tile_rows(ref, at, count, tile_len):
    at = jnp.clip(at, 0, count - 1)
    return lambda: ref[pl.ds(pl.multiple_of(at * tile_len, tile_len), tile_len), :]


def sort_lists(listed, counts, place, tiles_here, heads, reach):
    slots = listed.shape[1] // tiles_here

    def kernel(place_ref, listed_ref, counts_ref, inside_ref, halo_ref):
        first_head = place_ref[0]
        first_tile = place_ref[1]

        @pl.loop(0, heads)
        def _(head):
            @pl.loop(0, tiles_here)
            def _(tile):
                line = head * tiles_here + tile
                limit = counts_ref[first_head + head, tile]
                for spare in range(OWN_SLOTS):
                    inside_ref[line, spare] = 0
                for spare in range(HALO_SLOTS):
                    halo_ref[line, spare] = 0
                inside = jnp.int32(0)
                outside = jnp.int32(0)
                for slot in range(slots):
                    at = listed_ref[first_head + head, tile * slots + slot] - first_tile
                    is_inside = (at >= 0) & (at < tiles_here)
                    active = slot < limit

                    @pl.when(active & is_inside)
                    def _():
                        inside_ref[line, inside] = at

                    @pl.when(active & ~is_inside)
                    def _():
                        halo_ref[line, jnp.minimum(outside, HALO_SLOTS - 2)] = jnp.where(
                            at < 0, at + reach, at - tiles_here + reach
                        )

                    inside = inside + (active & is_inside).astype(jnp.int32)
                    outside = outside + (active & ~is_inside).astype(jnp.int32)
                inside_ref[line, OWN_SLOTS - 1] = inside
                halo_ref[line, HALO_SLOTS - 1] = outside

    smem = pl.BlockSpec(memory_space=pltpu.SMEM)
    lines = heads * tiles_here
    return pl.pallas_call(
        kernel,
        in_specs=[smem, smem, smem],
        out_specs=[smem, smem],
        out_shape=[
            jax.ShapeDtypeStruct((lines, OWN_SLOTS), jnp.int32),
            jax.ShapeDtypeStruct((lines, HALO_SLOTS), jnp.int32),
        ],
    )(place, listed, counts)


def tiles_of_step(step, tiles_here):
    first = [STEP_TILES // 2 * step + number for number in range(STEP_TILES // 2)]
    return first + [tiles_here - 1 - tile for tile in first]


def most_of(limits):
    most = limits[0]
    for limit in limits[1:]:
        most = jnp.maximum(most, limit)
    return most


def attend_local(own, query, inside, tile_len):
    sources, _, heads, tokens, head_dim = own.shape
    rows = sources * tokens
    tiles_here = rows // tile_len
    slots = tiles_here
    factor = math.log2(math.e) / math.sqrt(head_dim)

    def kernel(inside_ref, own_ref, query_ref, mixed_ref, stats_ref, buf, sems):
        def copies(head):
            pairs = [(own_ref, 0), (own_ref, 1), (query_ref, 0)]
            return [
                pltpu.make_async_copy(
                    ref.at[:, index, head], buf.at[number, head], sems.at[head, number]
                )
                for number, (ref, index) in enumerate(pairs)
            ]

        for head in range(heads):
            for copy in copies(head):
                copy.start()

        @pl.loop(0, heads)
        def _(head):
            for copy in copies(head):
                copy.wait()
            key_rows, value_rows, query_rows = [
                buf.at[number, head].reshape(rows, head_dim) for number in range(3)
            ]
            column = pl.ds(pl.multiple_of(head * head_dim, head_dim), head_dim)

            @pl.loop(0, tiles_here // STEP_TILES)
            def _(step):
                tiles = tiles_of_step(step, tiles_here)
                lines = [head * tiles_here + tile for tile in tiles]
                limits = [inside_ref[line, OWN_SLOTS - 1] for line in lines]
                most = most_of(limits)

                def work(used):
                    begun = []
                    for line, tile, limit in zip(lines, tiles, limits):
                        here = pl.ds(pl.multiple_of(tile * tile_len, tile_len), tile_len)
                        places = [inside_ref[line, slot] for slot in range(used)]
                        scores, largest = scores_of(
                            query_rows[here, :],
                            [tile_rows(key_rows, at, tiles_here, tile_len) for at in places],
                            limit,
                            1,
                        )
                        peak = jnp.max(largest, axis=1, keepdims=True) * factor
                        begun.append((here, places, scores, peak))
                    for here, places, scores, peak in begun:
                        total, mixed = mix(
                            scores,
                            peak,
                            factor,
                            [tile_rows(value_rows, at, tiles_here, tile_len) for at in places],
                        )
                        mixed_ref[here, column] = mixed / total
                        stats_ref[here, column] = jnp.broadcast_to(
                            peak + jnp.log2(total), (tile_len, head_dim)
                        )

                for used in range(2, slots + 1, 2):
                    @pl.when((most + 1) // 2 == used // 2)
                    def _():
                        work(used)

    smem = pl.BlockSpec(memory_space=pltpu.SMEM)
    hbm = pl.BlockSpec(memory_space=pl.ANY)
    vmem = pl.BlockSpec(memory_space=pltpu.VMEM)
    pairs = heads * tiles_here * slots
    state = jax.ShapeDtypeStruct((rows, heads * head_dim), jnp.float32)
    return pl.pallas_call(
        kernel,
        in_specs=[smem, hbm, hbm],
        out_specs=[vmem, vmem],
        out_shape=[state, state],
        scratch_shapes=[
            pltpu.VMEM((3, heads, sources, tokens, head_dim), jnp.bfloat16),
            pltpu.SemaphoreType.DMA((heads, 3)),
        ],
        compiler_params=pltpu.CompilerParams(vmem_limit_bytes=VMEM_BYTES // 3),
        cost_estimate=pl.CostEstimate(
            flops=4 * pairs * tile_len * tile_len * head_dim,
            bytes_accessed=2 * heads * head_dim * 7 * rows,
            transcendentals=pairs * tile_len * tile_len,
        ),
    )(inside, own, query)


def attend_halo(query, outer, inner, crossed, mixed, stats, halo, kinds, tile_len):
    sources, _, heads, tokens, head_dim = query.shape
    half = inner.shape[0]
    rows = sources * tokens
    halo_rows = 2 * half * tokens
    halo_tiles = halo_rows // tile_len
    reach = halo_tiles // 2
    tiles_here = rows // tile_len
    factor = math.log2(math.e) / math.sqrt(head_dim)
    needs = [max(reach - tile, tile - tiles_here + 1 + reach) for tile in range(tiles_here)]

    def kernel(halo_ref, kinds_ref, query_ref, outer_k, outer_v, crossed_k, crossed_v, inner_ref,
               mixed_ref, stats_ref, out_ref, buf, sems):
        def query_tile(head, tile):
            pieces = []
            at = tile * tile_len
            while at < (tile + 1) * tile_len:
                source, row = divmod(at, tokens)
                length = min(tokens - row, (tile + 1) * tile_len - at)
                pieces.append(query_ref[source, 0, head, row : row + length, :])
                at += length
            return jnp.concatenate(pieces, axis=0) if len(pieces) > 1 else pieces[0]

        def side_copy(head, index, side, kind):
            if kind == INNER:
                source = inner_ref.at[:, index, head]
            elif kind == OUTER:
                source = (outer_k, outer_v)[index].at[:, head]
            else:
                source = (crossed_k, crossed_v)[index].at[:, head]
            return pltpu.make_async_copy(
                source,
                buf.at[index, head, pl.ds(side * half, half)],
                sems.at[head, 2 * index + side],
            )

        for head in range(heads):
            for side in range(2):
                for kind in (INNER, OUTER, CROSSED):
                    @pl.when(kinds_ref[side] == kind)
                    def _():
                        for index in range(2):
                            side_copy(head, index, side, kind).start()

        @pl.loop(0, heads)
        def _(head):
            for side in range(2):
                side_copy(head, 0, side, INNER).wait()
            key_rows, value_rows = [
                buf.at[index, head].reshape(halo_rows, head_dim) for index in range(2)
            ]
            column = pl.ds(pl.multiple_of(head * head_dim, head_dim), head_dim)
            lines = [head * tiles_here + tile for tile in range(tiles_here)]
            limits = [halo_ref[line, HALO_SLOTS - 1] for line in lines]
            most = most_of(limits)

            def work(cap):
                begun = []
                for tile in range(tiles_here):
                    here = slice(tile * tile_len, (tile + 1) * tile_len)
                    used = min(cap, needs[tile] + needs[tile] % 2)
                    if not used:
                        out_ref[here, column] = mixed_ref[here, column].astype(jnp.bfloat16)
                        continue
                    places = [halo_ref[lines[tile], slot] for slot in range(used)]
                    scores, largest = scores_of(
                        query_tile(head, tile),
                        [tile_rows(key_rows, at, halo_tiles, tile_len) for at in places],
                        limits[tile],
                        0,
                    )
                    level = stats_ref[here, column]
                    newest = jnp.maximum(level, jnp.max(largest, axis=1, keepdims=True) * factor)
                    begun.append((here, places, scores, newest, jnp.exp2(level - newest)))
                for side in range(2):
                    side_copy(head, 1, side, INNER).wait()
                for here, places, scores, newest, fade in begun:
                    added, update = mix(
                        scores,
                        newest,
                        factor,
                        [tile_rows(value_rows, at, halo_tiles, tile_len) for at in places],
                    )
                    out_ref[here, column] = (
                        (mixed_ref[here, column] * fade + update) / (fade + added)
                    ).astype(jnp.bfloat16)

            for cap in range(0, HALO_SLOTS - 1, 2):
                @pl.when((most + 1) // 2 == cap // 2)
                def _():
                    work(cap)

    smem = pl.BlockSpec(memory_space=pltpu.SMEM)
    hbm = pl.BlockSpec(memory_space=pl.ANY)
    vmem = pl.BlockSpec(memory_space=pltpu.VMEM)
    pairs = heads * tiles_here * (HALO_SLOTS - 2) // 2
    return pl.pallas_call(
        kernel,
        in_specs=[smem, smem, vmem] + [hbm] * 5 + [vmem, vmem],
        out_specs=vmem,
        out_shape=jax.ShapeDtypeStruct((rows, heads * head_dim), jnp.bfloat16),
        scratch_shapes=[
            pltpu.VMEM((2, heads, 2 * half, tokens, head_dim), jnp.bfloat16),
            pltpu.SemaphoreType.DMA((heads, 4)),
        ],
        compiler_params=pltpu.CompilerParams(vmem_limit_bytes=VMEM_BYTES // 3),
        cost_estimate=pl.CostEstimate(
            flops=4 * pairs * tile_len * tile_len * head_dim,
            bytes_accessed=2 * heads * head_dim * (2 * halo_rows + 6 * rows),
            transcendentals=pairs * tile_len * tile_len,
        ),
    )(halo, kinds, query, *outer, *crossed, inner, mixed, stats)


def routes(blocks, group_size):
    def on(block):
        there = block + 1
        if there % ROW == 0:
            there = block + 1 - ROW if odd_row(block) == 0 else block + 1 + ROW
        return there

    def back(block):
        there = block - 1
        if block % ROW == 0:
            there = block - 1 + ROW if odd_row(block) == 1 else block - 1 - ROW
        return there

    outer, inner, across = [], [], []
    for block in range(blocks):
        odd_place = block % 2 == 1
        for pairs, there in (
            (outer, on(block) if odd_place else back(block)),
            (inner, back(block) if odd_place else on(block)),
        ):
            if 0 <= there < blocks:
                pairs += [(block * group_size + m, there * group_size + m) for m in range(group_size)]
        if block % ROW in (0, ROW - 1):
            other = block + ROW if odd_row(block) == 0 else block - ROW
            across += [
                tuple(at * group_size + owner_of(at, head_block, group_size) for at in (block, other))
                for head_block in range(group_size)
            ]
    return outer, inner, across


def assemble(parts):
    members, tokens, width = parts.shape
    step = tokens // 2

    def kernel(parts_ref, out_ref):
        odd = odd_row(lax.axis_index("seq"))
        first = pl.multiple_of(pl.program_id(0) * step, step)
        for member in range(members):
            column = pl.multiple_of(owner_block(member, odd, members) * width, width)
            out_ref[:, pl.ds(column, width)] = parts_ref[member, pl.ds(first, step), :]

    return pl.pallas_call(
        kernel,
        grid=(tokens // step,),
        in_specs=[pl.BlockSpec(memory_space=pltpu.VMEM)],
        out_specs=pl.BlockSpec((step, members * width), lambda g: (g, 0)),
        out_shape=jax.ShapeDtypeStruct((tokens, members * width), parts.dtype),
        compiler_params=pltpu.CompilerParams(vmem_limit_bytes=VMEM_BYTES // 3),
        cost_estimate=pl.CostEstimate(
            flops=0, bytes_accessed=4 * tokens * members * width, transcendentals=0
        ),
    )(parts)


def body(queries, keys, values, neighbours, counts):
    group_size = lax.axis_size("head")
    blocks = lax.axis_size("seq")
    local_tokens, feature_width = queries.shape
    head_count, tiles_here = counts.shape
    head_dim = feature_width // head_count
    per_device = head_count // group_size
    tile_len = local_tokens * group_size // tiles_here
    half = group_size // 2
    halo_tiles = half * local_tokens // tile_len

    def exchange(array):
        return lax.all_to_all(array, "head", split_axis=0, concat_axis=0, tiled=True)

    own = exchange(prepare([keys, values], [True, False], group_size, per_device, head_dim))
    block = lax.axis_index("seq")
    head_block = owner_block(lax.axis_index("head"), odd_row(block), group_size)
    place = jnp.stack([head_block * per_device, block * tiles_here]).astype(jnp.int32)
    x = block % ROW
    odd_place = x % 2 == 1
    kinds = jnp.stack(
        [
            jnp.where(odd_place, INNER, jnp.where(x == 0, CROSSED, OUTER)),
            jnp.where(odd_place, jnp.where(x == ROW - 1, CROSSED, OUTER), INNER),
        ]
    ).astype(jnp.int32)
    listed = neighbours.reshape(head_count, -1)
    inside, halo = sort_lists(listed, counts, place, tiles_here, per_device, halo_tiles)
    queries, inside, halo, kinds = lax.optimization_barrier((queries, inside, halo, kinds))
    query = exchange(prepare([queries], [True], group_size, per_device, head_dim))
    outer_route, inner_route, across = routes(blocks, group_size)
    both = ("seq", "head")
    first = jnp.where(odd_place, half, 0)
    outer_part = lax.dynamic_slice_in_dim(own, first, half, 0)
    inner_part = lax.dynamic_slice_in_dim(own, half - first, half, 0)
    outer = [lax.ppermute(outer_part[:, index], both, outer_route) for index in range(2)]
    inner = lax.ppermute(inner_part, both, inner_route)
    crossed = [lax.ppermute(part, both, across) for part in outer]
    mixed, stats = attend_local(own, query, inside, tile_len)
    result = attend_halo(query, outer, inner, crossed, mixed, stats, halo, kinds, tile_len)
    result = exchange(result.reshape(group_size, local_tokens, per_device * head_dim))
    return assemble(result)


def solution(mesh):
    placed = (
        P(("seq", "head"), None),
        P(("seq", "head"), None),
        P(("seq", "head"), None),
        P(None, "seq", None),
        P(None, "seq"),
    )
    return jax.shard_map(
        body, mesh=mesh, in_specs=placed, out_specs=P(("seq", "head"), None), check_vma=False
    )
```
